256 devices in a mesh: az: 32 (over y, z), rg: 8 (over x, core).
Axes of the slice: x: 4, y: 4, z: 8, core: 2. Of those that a mesh axis runs over, the one named last changes fastest.
Arguments:
- echo_field: float32 [2, 2048, 8192], P(None, 'az', 'rg'), may hold values from -6 to 6
- range_chirp: bfloat16 [2, 2048], replicated, may hold values from -0.25 to 0.25
- azimuth_filter: float32 [2, 2048, 8192], P(None, 'az', 'rg'), may hold values from -5 to 5
- shifts: int32 [2048], P('az'), may hold values from 0 to 2040, as said below
- tap_index: int32 [2048], P('az'), may hold values from 0 to 15
- taps_table: float32 [16, 8], replicated, may hold values from -2 to 2
Outputs:
- focused_image: float32 [2, 2048, 8192], P(None, 'az', 'rg')
The draws below stay inside these ranges and needn't reach their ends.
Inputs may be any that keep to these rules, and one draw needn't show every extreme that they name: Within each aligned block of 64 rows at most 32 shifts are 1024 or more, and some block has exactly 32; a shift below 1024 is at most 1016, any other at most 2040.
All inputs are finite; a program needn't handle non-finite values.
Results may differ from the reference program's by a relative error of at most 0.0029.
Values may be sent and summed in bfloat16 or wider, within the bound.
A program may use at most 128 MiB of HBM per device.

```python
import jax
import jax.numpy as jnp
import numpy as np
from jax import lax

AZ_DEV = 64
RANGE_DEV = 1024
CHIRP = 2048
TAPS = 8
PHASES = 16
CAPACITY = 32
AZIMUTH_ROWS = 2048
RANGE_CELLS = 8192
N_AZ = 32


def draw_shifts(key, part):
    key = jax.random.fold_in(key, 11)
    key_count, key_pick, key_perm, key_rest = jax.random.split(key, 4)
    block_total = AZIMUTH_ROWS // AZ_DEV
    counts = jax.random.randint(key_count, (block_total,), 0, CAPACITY + 1)
    chosen = jax.random.randint(key_pick, (), 0, block_total)
    block_ids = jnp.arange(block_total)
    counts = jnp.where(block_ids == chosen, CAPACITY, counts)
    perm_keys = jax.random.split(key_perm, block_total)
    row_rank = jax.vmap(lambda one_key: jax.random.permutation(one_key, AZ_DEV))(perm_keys)
    distant = (row_rank < counts[:, None]).astype(jnp.int32)
    remainder = jax.random.randint(key_rest, (block_total, AZ_DEV), 0, RANGE_DEV - 7)
    in_chosen = (block_ids == chosen)[:, None]
    remainder = jnp.where(in_chosen & (row_rank == 0), RANGE_DEV - 8, remainder)
    remainder = jnp.where(in_chosen & (row_rank == AZ_DEV - 1), 0, remainder)
    return (distant * RANGE_DEV + remainder).reshape(AZIMUTH_ROWS).astype(jnp.int32)


def with_ends(values, own_key, low, largest):
    place = [jax.random.randint(jax.random.fold_in(own_key, axis), (), 0, length) for axis, length in enumerate(values.shape)]
    widest = values.shape.index(max(values.shape))
    next_to = place[:widest] + [(place[widest] + 1) % values.shape[widest]] + place[widest + 1:]
    return values.at[tuple(place)].set(low).at[tuple(next_to)].set(largest)


def block_scale(key, extent, shards, least, top_value):
    def one(dim, parts):
        steps = jax.random.uniform(jax.random.fold_in(jax.random.fold_in(key, 6), dim), (parts,), jnp.float32, least / len(shards), top_value / len(shards))
        return jnp.repeat(jnp.exp(steps), extent[dim] // parts).reshape((-1,) + (1,) * (len(extent) - dim - 1))

    factor_of = one(*shards[0])
    for cut in shards[1:]:
        factor_of = factor_of * one(*cut)
    return factor_of


def normal_values(stream_key, dims, width, reach, cuts=(), dtype=jnp.bfloat16):
    array = width * jax.random.normal(stream_key, dims, jnp.float32)
    if cuts:
        array = array * block_scale(stream_key, dims, cuts, -0.22, 0.18)
    return jnp.clip(array, -reach, reach).astype(dtype)


def setup_inputs(seed: int = 0) -> dict:
    key_list = jax.random.split(jax.random.key(seed), 7)
    return {
        "echo_field": normal_values(key_list[0], (2, AZIMUTH_ROWS, RANGE_CELLS), 1.0, 6.0, ((1, 32), (2, 8)), jnp.float32),
        "range_chirp": normal_values(key_list[1], (2, CHIRP), ((2 * CHIRP) ** -0.5), 0.25),
        "azimuth_filter": normal_values(key_list[2], (2, AZIMUTH_ROWS, RANGE_CELLS), 0.7, 5.0, ((1, 32), (2, 8)), jnp.float32),
        "shifts": draw_shifts(jax.random.fold_in(key_list[6], 71), 0),
        "tap_index": with_ends(jax.random.randint(key_list[4], (AZIMUTH_ROWS,), 0, PHASES), jax.random.fold_in(key_list[4], 1), 0, PHASES - 1).astype(jnp.int32),
        "taps_table": normal_values(key_list[5], (PHASES, TAPS), 0.35, 2.0, (), jnp.float32),
    }


def reverse_bits(value, width_bits):
    result = value * 0
    for position in range(width_bits):
        result = result + (((value >> position) & 1) << (width_bits - 1 - position))
    return result


def stored_order():
    levels = N_AZ.bit_length() - 1
    row_ids = np.arange(AZIMUTH_ROWS)
    return reverse_bits(row_ids // AZ_DEV, levels) + N_AZ * (row_ids % AZ_DEV)


def reference(echo_field, range_chirp, azimuth_filter, shifts, tap_index, taps_table):
    echo_low = lax.optimization_barrier(echo_field.astype(jnp.bfloat16)).astype(jnp.float32)
    signal = echo_low[0] + 1j * echo_low[1]
    chirp_wide = range_chirp.astype(jnp.float32)
    taps_complex = chirp_wide[0] + 1j * chirp_wide[1]
    padded_length = RANGE_CELLS + CHIRP
    product = jnp.fft.fft(signal, n=padded_length, axis=1) * jnp.fft.fft(taps_complex[::-1], n=padded_length)[None, :]
    compressed = jnp.fft.ifft(product, axis=1)[:, CHIRP - 1:CHIRP - 1 + RANGE_CELLS]
    azimuth_spectrum = jnp.fft.fft(compressed, axis=0, norm="ortho")
    row_order = stored_order()
    spec_real = jnp.real(azimuth_spectrum)[row_order]
    spec_imag = jnp.imag(azimuth_spectrum)[row_order]
    spectrum = jnp.stack([spec_real, spec_imag], axis=1)
    coefficients = taps_table[tap_index]
    padded = jnp.pad(spectrum, ((0, 0), (0, 0), (0, 2 * RANGE_DEV)))

    def migrate_row(row_items):
        row_data, start_cell, weights = row_items
        window = lax.dynamic_slice_in_dim(row_data, start_cell, RANGE_CELLS + TAPS - 1, 1)
        total = weights[0] * window[:, 0:RANGE_CELLS]
        for tap_number in range(1, TAPS):
            total = total + weights[tap_number] * window[:, tap_number:tap_number + RANGE_CELLS]
        return total

    migrated = lax.map(migrate_row, (padded, shifts.astype(jnp.int32), coefficients))
    filt_real = migrated[:, 0] * azimuth_filter[0] - migrated[:, 1] * azimuth_filter[1]
    filt_imag = migrated[:, 0] * azimuth_filter[1] + migrated[:, 1] * azimuth_filter[0]
    inverse_order = np.argsort(row_order)
    natural = filt_real[inverse_order] + 1j * filt_imag[inverse_order]
    focused = jnp.fft.ifft(natural, axis=0, norm="ortho")
    return jnp.stack([jnp.real(focused), jnp.imag(focused)])
```

```python
import functools
import math

import jax
import jax.numpy as jnp
import numpy as np
from jax import lax
from jax.experimental import pallas as pl
from jax.experimental.pallas import tpu as pltpu
from jax.sharding import PartitionSpec as P

MESH = pl.DeviceIdType.MESH
F32 = jnp.float32
BF16 = jnp.bfloat16
LANE = 128
SUB = 16


def encode(x):
    return (x * jnp.abs(x)).astype(BF16)


def decode(code):
    c = code.astype(F32)
    return c * lax.rsqrt(jnp.maximum(jnp.abs(c), 1e-37))


def bit_reverse(value, bits):
    result = 0
    for position in range(bits):
        result += ((value >> position) & 1) << (bits - 1 - position)
    return result


def turn(pair, k, n, sign):
    re, im = pair
    if k == 0:
        return re, im
    if 4 * k == n:
        return (-im, re) if sign > 0 else (im, -re)
    c = math.cos(2 * math.pi * k / n)
    s = sign * math.sin(2 * math.pi * k / n)
    if 8 * k == n:
        return ((re - im) * c, (re + im) * c) if sign > 0 else ((re + im) * c, (im - re) * c)
    if 8 * k == 3 * n:
        h = -c
        return (-(re + im) * h, (re - im) * h) if sign > 0 else ((im - re) * h, -(re + im) * h)
    return re * c - im * s, re * s + im * c


def fft_forward(xs):
    n = len(xs)
    if n == 1:
        return xs
    half = n // 2
    low, high = [], []
    for k in range(half):
        (ar, ai), (br, bi) = xs[k], xs[k + half]
        low.append((ar + br, ai + bi))
        high.append(turn((ar - br, ai - bi), k, n, -1))
    return fft_forward(low) + fft_forward(high)


def fft_inverse(xs):
    n = len(xs)
    if n == 1:
        return xs
    half = n // 2
    low = fft_inverse(xs[:half])
    high = fft_inverse(xs[half:])
    first, second = [], []
    for k in range(half):
        ar, ai = low[k]
        br, bi = turn(high[k], k, n, 1)
        first.append((ar + br, ai + bi))
        second.append((ar - br, ai - bi))
    return first + second


def trig_tables(n_az, rows):
    total = n_az * rows
    bits = n_az.bit_length() - 1
    tables = np.zeros((n_az, 4, 2 * rows, 2 * rows), np.float32)
    s = np.arange(rows)[None, :]
    j = np.arange(rows)[:, None]
    for p in range(n_az):
        b = bit_reverse(p, bits)
        angle = 2 * np.pi * ((s * (b + n_az * j)) % total) / total
        c, d = np.cos(angle) / math.sqrt(rows), np.sin(angle) / math.sqrt(rows)
        m = np.block([[c, d], [-d, c]])
        for at, mat in ((0, m), (2, m.T)):
            high = mat.astype(np.float32).astype(jnp.bfloat16)
            tables[p, at] = high.astype(np.float32)
            tables[p, at + 1] = mat - high.astype(np.float64)
    return tables.astype(jnp.bfloat16)


def kernel(
    n,
    ng,
    chirp_len,
    echo,
    chirp,
    filt_hbm,
    shifts,
    tap_index,
    table,
    trig_hbm,
    out,
    filt,
    trig,
    band,
    weights,
    wide,
    send_1,
    recv_1,
    work,
    send_2,
    recv_2,
    spec,
    spec_code,
    halo_1,
    halo_2,
    high,
    low,
    send_3,
    recv_3,
    send_4,
    recv_4,
    local_sem,
    halo_send,
    halo_recv,
    az_send,
    az_recv,
):
    rows, cells = echo.shape[1], echo.shape[2]
    me = lax.axis_index("az")
    g = lax.axis_index("rg")
    lanes = cells // LANE
    block = min(256, cells)

    barrier = pltpu.get_barrier_semaphore()

    def greet(k, carry):
        pl.semaphore_signal(
            barrier, inc=1, device_id=(lax.rem(me + k, n), g), device_id_type=MESH
        )
        return carry

    lax.fori_loop(1, n, greet, 0)
    for d in (1, 2, ng - 2, ng - 1):
        pl.semaphore_signal(barrier, inc=1, device_id=(me, lax.rem(g + d, ng)), device_id_type=MESH)

    filt_copy = pltpu.make_async_copy(filt_hbm, filt, local_sem.at[0])
    filt_copy.start()
    trig_copy = pltpu.make_async_copy(trig_hbm.at[me], trig, local_sem.at[1])
    trig_copy.start()

    wide[:, 0:cells] = echo[...].reshape(2 * rows, cells).astype(BF16)

    span = chirp_len + 2 * block
    row_id = lax.broadcasted_iota(jnp.int32, (LANE, LANE), 0)
    col_id = lax.broadcasted_iota(jnp.int32, (LANE, LANE), 1)
    mirror = (row_id + col_id == LANE - 1).astype(BF16)
    pieces = [
        jnp.dot(chirp[:, LANE * i : LANE * (i + 1)], mirror, preferred_element_type=F32)
        for i in reversed(range(chirp_len // LANE))
    ]
    edge = jnp.zeros((2, block), F32)
    base = jnp.concatenate([edge] + pieces + [edge], axis=1)
    for c in range(2):
        spread = jnp.broadcast_to(base[c : c + 1], (LANE, span))
        band[c] = pltpu.roll(spread, 1, 1, stride=1, stride_axis=0).astype(BF16)

    pl.semaphore_wait(barrier, n - 1 + 4)

    def halo_copy(src, dst, slot, d):
        return pltpu.make_async_remote_copy(
            src_ref=src,
            dst_ref=dst,
            send_sem=halo_send.at[slot],
            recv_sem=halo_recv.at[slot],
            device_id=(me, lax.rem(g - d + ng, ng)),
            device_id_type=MESH,
        )

    echo_copies = [
        halo_copy(wide.at[:, pl.ds(0, cells)], wide.at[:, pl.ds(d * cells, cells)], d - 1, d)
        for d in (1, 2)
    ]
    for d in (1, 2):
        pl.when(g >= d)(echo_copies[d - 1].start)

    for a in range((chirp_len + block) // LANE):
        start = chirp_len + block - LANE * a
        for c in range(2):
            weights[LANE * a : LANE * (a + 1), block * c : block * (c + 1)] = band[
                c, :, start : start + block
            ]

    for d in (1, 2):
        pl.when(g + d < ng)(echo_copies[d - 1].wait_recv)

        @pl.when(g + d >= ng)
        def _(d=d):
            wide[:, d * cells : (d + 1) * cells] = jnp.zeros((2 * rows, cells), BF16)

    for m in range(cells // block):
        left = wide[:, block * m : block * m + chirp_len + block]
        product = jnp.dot(left, weights[...], preferred_element_type=F32)
        real = product[:rows, :block] - product[rows:, block:]
        imag = product[:rows, block:] + product[rows:, :block]
        send_1[0, :, block * m : block * (m + 1)] = encode(real)
        send_1[1, :, block * m : block * (m + 1)] = encode(imag)

    def tile(ref, q):
        row = pl.multiple_of(SUB * lax.div(q, lanes), SUB)
        col = pl.multiple_of(LANE * lax.rem(q, lanes), LANE)
        return ref.at[:, pl.ds(row, SUB), pl.ds(col, LANE)]

    def scatter_copy(src, dst, phase, q):
        return pltpu.make_async_remote_copy(
            src_ref=tile(src, q),
            dst_ref=dst.at[me],
            send_sem=az_send.at[phase, q],
            recv_sem=az_recv.at[phase, me],
            device_id=(q, g),
            device_id_type=MESH,
        )

    def gather_copy(src, dst, phase, q):
        return pltpu.make_async_remote_copy(
            src_ref=src.at[q],
            dst_ref=tile(dst, me),
            send_sem=az_send.at[phase, q],
            recv_sem=az_recv.at[phase, me],
            device_id=(q, g),
            device_id_type=MESH,
        )

    def exchange(make, src, dst, phase, own_src, own_dst, landing):
        own = pltpu.make_async_copy(own_src, own_dst, local_sem.at[2 + phase])
        own.start()

        def start(k, carry):
            make(src, dst, phase, lax.rem(me + k, n)).start()
            return carry

        lax.fori_loop(1, n, start, 0)

        def arrive(k, carry):
            q = lax.rem(me + k, n)
            pltpu.make_async_remote_copy(
                src_ref=landing(q),
                dst_ref=landing(q),
                send_sem=az_send.at[phase, q],
                recv_sem=az_recv.at[phase, q],
                device_id=(q, g),
                device_id_type=MESH,
            ).wait_recv()
            return carry

        lax.fori_loop(1, n, arrive, 0)
        own.wait()

    def scatter(src, dst, phase):
        exchange(
            scatter_copy, src, dst, phase, tile(src, me), dst.at[me], lambda q: dst.at[q]
        )

    def gather(src, dst, phase):
        exchange(
            gather_copy, src, dst, phase, src.at[me], tile(dst, me), lambda q: tile(dst, q)
        )

    def transform(fft, src, dst):
        work[...] = decode(src[...])

        def half(h, carry):
            at = pl.ds(pl.multiple_of(8 * h, 8), 8)
            xs = [(work[p, 0, at, :], work[p, 1, at, :]) for p in range(n)]
            for p, (re, im) in enumerate(fft(xs)):
                work[p, 0, at, :] = re
                work[p, 1, at, :] = im
            return carry

        lax.fori_loop(0, SUB // 8, half, 0)
        dst[...] = encode(work[...] * (1.0 / math.sqrt(n)))

    scatter(send_1, recv_1, 0)
    transform(fft_forward, recv_1, send_2)
    gather(send_2, recv_2, 1)

    trig_copy.wait()
    values = decode(recv_2[...]).reshape(2 * rows, cells)
    value_high = values.astype(BF16)
    value_low = (values - value_high.astype(F32)).astype(BF16)
    spectrum = jnp.dot(
        jnp.concatenate([trig[0], trig[1], trig[0]], axis=1),
        jnp.concatenate([value_high, value_high, value_low], axis=0),
        preferred_element_type=F32,
    )
    spec[...] = spectrum
    spec_code[...] = encode(spectrum)
    spec_copies = [halo_copy(spec_code, (halo_1, halo_2)[d - 1], d + 1, d) for d in (1, 2)]
    for d in (1, 2):
        pl.when(g >= d)(spec_copies[d - 1].start)

    def upright(values_1d):
        across = jnp.broadcast_to(values_1d.astype(F32).reshape(1, rows), (rows, rows))
        on_row = lax.broadcasted_iota(jnp.int32, (rows, rows), 0)
        on_col = lax.broadcasted_iota(jnp.int32, (rows, rows), 1)
        return jnp.sum(jnp.where(on_row == on_col, across, 0.0), axis=1, keepdims=True)

    shift_col = upright(shifts[...])
    index_col = upright(tap_index[...])
    phases, taps = table.shape
    coefs = jnp.zeros((rows, taps), F32)
    for phase in range(phases):
        coefs = coefs + jnp.where(index_col == float(phase), table[phase : phase + 1, :], 0.0)

    for d in (1, 2):
        pl.when(g + d < ng)(spec_copies[d - 1].wait_recv)

        @pl.when(g + d >= ng)
        def _(d=d):
            (halo_1, halo_2)[d - 1][...] = jnp.zeros((2 * rows, cells), BF16)

    filt_copy.wait()

    top = cells // 2
    for r0 in range(0, rows, SUB):
        shift = shift_col[r0 : r0 + SUB]
        distant = shift >= float(cells)
        rest = jnp.where(distant, shift - float(cells), shift)
        bits = []
        step = top
        while step >= 1:
            bit = rest >= float(step)
            rest = jnp.where(bit, rest - float(step), rest)
            bits.append((step, bit))
            step //= 2
        parts = []
        for c in range(2):
            at = slice(c * rows + r0, c * rows + r0 + SUB)
            near = decode(halo_1[at, :])
            far = decode(halo_2[at, :])
            cur = jnp.concatenate(
                [
                    jnp.where(distant, near, spec[at, :]),
                    jnp.where(distant, far, near),
                    jnp.zeros((SUB, LANE), F32),
                ],
                axis=1,
            )
            for step, bit in bits:
                if step >= LANE:
                    width = cells + step + LANE
                    cur = jnp.where(bit, cur[:, step : step + width], cur[:, :width])
                else:
                    width = cells + 2 * LANE
                    cur = jnp.where(bit, pltpu.roll(cur, width - step, 1), cur)
            total = coefs[r0 : r0 + SUB, 0:1] * cur[:, :cells]
            for q in range(1, taps):
                cur = pltpu.roll(cur, width - 1, 1)
                total = total + coefs[r0 : r0 + SUB, q : q + 1] * cur[:, :cells]
            parts.append(total)
        fr = filt[0, r0 : r0 + SUB, :]
        fi = filt[1, r0 : r0 + SUB, :]
        both = (parts[0] * fr - parts[1] * fi, parts[0] * fi + parts[1] * fr)
        for c in range(2):
            at = slice(c * rows + r0, c * rows + r0 + SUB)
            rounded = both[c].astype(BF16)
            high[at, :] = rounded
            low[at, :] = (both[c] - rounded.astype(F32)).astype(BF16)

    inverse = jnp.dot(
        jnp.concatenate([trig[2], trig[3], trig[2]], axis=1),
        jnp.concatenate([high[...], high[...], low[...]], axis=0),
        preferred_element_type=F32,
    )
    send_3[...] = encode(inverse).reshape(2, rows, cells)

    scatter(send_3, recv_3, 2)
    transform(fft_inverse, recv_3, send_4)
    gather(send_4, recv_4, 3)
    out[...] = decode(recv_4[...])

    for d in (1, 2):
        pl.when(g >= d)(echo_copies[d - 1].wait_send)
        pl.when(g >= d)(spec_copies[d - 1].wait_send)

    def drain(k, carry):
        q = lax.rem(me + k, n)
        scatter_copy(send_1, recv_1, 0, q).wait_send()
        gather_copy(send_2, recv_2, 1, q).wait_send()
        scatter_copy(send_3, recv_3, 2, q).wait_send()
        gather_copy(send_4, recv_4, 3, q).wait_send()
        return carry

    lax.fori_loop(1, n, drain, 0)


def solution(mesh):
    n, ng = mesh.shape["az"], mesh.shape["rg"]

    def local(echo_field, range_chirp, azimuth_filter, shifts, tap_index, taps_table):
        rows, cells = echo_field.shape[1], echo_field.shape[2]
        chirp_len = range_chirp.shape[1]
        block = min(256, cells)
        trig = jnp.asarray(trig_tables(n, rows))
        stack = (2, rows, cells)
        flat = (2 * rows, cells)
        tiles = (n, 2, SUB, LANE)
        vmem = pl.BlockSpec(memory_space=pltpu.VMEM)
        hbm = pl.BlockSpec(memory_space=pl.ANY)
        return pl.pallas_call(
            functools.partial(kernel, n, ng, chirp_len),
            out_shape=jax.ShapeDtypeStruct(stack, F32),
            in_specs=[vmem, vmem, hbm, vmem, vmem, vmem, hbm],
            out_specs=vmem,
            scratch_shapes=[
                pltpu.VMEM(stack, F32),
                pltpu.VMEM((4, 2 * rows, 2 * rows), BF16),
                pltpu.VMEM((2, LANE, chirp_len + 2 * block), BF16),
                pltpu.VMEM((chirp_len + block, 2 * block), BF16),
                pltpu.VMEM((2 * rows, 3 * cells), BF16),
                pltpu.VMEM(stack, BF16),
                pltpu.VMEM(tiles, BF16),
                pltpu.VMEM(tiles, F32),
                pltpu.VMEM(tiles, BF16),
                pltpu.VMEM(stack, BF16),
                pltpu.VMEM(flat, F32),
                pltpu.VMEM(flat, BF16),
                pltpu.VMEM(flat, BF16),
                pltpu.VMEM(flat, BF16),
                pltpu.VMEM(flat, BF16),
                pltpu.VMEM(flat, BF16),
                pltpu.VMEM(stack, BF16),
                pltpu.VMEM(tiles, BF16),
                pltpu.VMEM(tiles, BF16),
                pltpu.VMEM(stack, BF16),
                pltpu.SemaphoreType.DMA((6,)),
                pltpu.SemaphoreType.DMA((4,)),
                pltpu.SemaphoreType.DMA((4,)),
                pltpu.SemaphoreType.DMA((4, n)),
                pltpu.SemaphoreType.DMA((4, n)),
            ],
            compiler_params=pltpu.CompilerParams(
                collective_id=0, has_side_effects=True, vmem_limit_bytes=48 * 1024 * 1024
            ),
            cost_estimate=pl.CostEstimate(
                flops=1_600_000_000, bytes_accessed=2_000_000, transcendentals=0
            ),
        )(echo_field, range_chirp, azimuth_filter, shifts, tap_index, taps_table, trig)

    placed = (P(None, "az", "rg"), P(), P(None, "az", "rg"), P("az"), P("az"), P())
    return jax.shard_map(
        local, mesh=mesh, in_specs=placed, out_specs=P(None, "az", "rg"), check_vma=False
    )
```

```python
import functools
import math

import jax
import jax.numpy as jnp
import numpy as np
from jax import lax
from jax.experimental import pallas as pl
from jax.experimental.pallas import tpu as pltpu
from jax.sharding import PartitionSpec as P

MESH = pl.DeviceIdType.MESH
F32 = jnp.float32
BF16 = jnp.bfloat16
LANE = 128
SUB = 16
HALF = 8
PARTS = 2
UNROLL = 4


def encode(x):
    return (x * jnp.abs(x)).astype(BF16)


def decode(code):
    c = code.astype(F32)
    return c * lax.rsqrt(jnp.maximum(jnp.abs(c), 1e-37))


def bit_reverse(value, bits):
    result = 0
    for position in range(bits):
        result += ((value >> position) & 1) << (bits - 1 - position)
    return result


def turn(pair, k, n, sign):
    re, im = pair
    if k == 0:
        return re, im
    if 4 * k == n:
        return (-im, re) if sign > 0 else (im, -re)
    c = math.cos(2 * math.pi * k / n)
    s = sign * math.sin(2 * math.pi * k / n)
    if 8 * k == n:
        return ((re - im) * c, (re + im) * c) if sign > 0 else ((re + im) * c, (im - re) * c)
    if 8 * k == 3 * n:
        h = -c
        return (-(re + im) * h, (re - im) * h) if sign > 0 else ((im - re) * h, -(re + im) * h)
    return re * c - im * s, re * s + im * c


def fft_forward(xs):
    n = len(xs)
    if n == 1:
        return xs
    half = n // 2
    low, high = [], []
    for k in range(half):
        (ar, ai), (br, bi) = xs[k], xs[k + half]
        low.append((ar + br, ai + bi))
        high.append(turn((ar - br, ai - bi), k, n, -1))
    return fft_forward(low) + fft_forward(high)


def fft_inverse(xs):
    n = len(xs)
    if n == 1:
        return xs
    half = n // 2
    low = fft_inverse(xs[:half])
    high = fft_inverse(xs[half:])
    first, second = [], []
    for k in range(half):
        ar, ai = low[k]
        br, bi = turn(high[k], k, n, 1)
        first.append((ar + br, ai + bi))
        second.append((ar - br, ai - bi))
    return first + second


def packed(rows):
    group, part, inner = np.meshgrid(
        np.arange(rows // HALF), np.arange(2), np.arange(HALF), indexing="ij"
    )
    return (part * rows + group * HALF + inner).reshape(-1)


def trig_tables(n_az, rows):
    total = n_az * rows
    bits = n_az.bit_length() - 1
    order = packed(rows)
    tables = np.zeros((n_az, 4, 2 * rows, 2 * rows), np.float32)
    s = np.arange(rows)[None, :]
    j = np.arange(rows)[:, None]
    for p in range(n_az):
        b = bit_reverse(p, bits)
        angle = 2 * np.pi * ((s * (b + n_az * j)) % total) / total
        c, d = np.cos(angle) / math.sqrt(rows), np.sin(angle) / math.sqrt(rows)
        m = np.block([[c, d], [-d, c]])[np.ix_(order, order)]
        for at, mat in ((0, m), (2, m.T)):
            high = mat.astype(np.float32).astype(jnp.bfloat16)
            tables[p, at] = high.astype(np.float32)
            tables[p, at + 1] = mat - high.astype(np.float64)
    return tables.astype(jnp.bfloat16)


def kernel(
    n,
    ng,
    slots,
    echo_hbm,
    chirp_hbm,
    filt_hbm,
    shifts_hbm,
    tap_index_hbm,
    table_hbm,
    trig_hbm,
    out,
    echo,
    chirp,
    filt,
    shifts,
    tap_index,
    table,
    trig,
    band,
    weights,
    wide,
    shift_wide,
    coef_wide,
    spread,
    gathering,
    send_1,
    recv_1,
    send_2,
    recv_2,
    spec,
    spec_code,
    far_code,
    halo_1,
    halo_2,
    high,
    low,
    send_3,
    recv_3,
    send_4,
    recv_4,
    local_sem,
    halo_send,
    halo_recv,
    az_send,
    az_recv,
):
    rows, cells = echo.shape[1], echo.shape[2]
    chirp_len = chirp.shape[1]
    part = cells // PARTS
    lanes = part // LANE
    groups = rows // HALF
    block = 256
    nz = 8
    me = lax.axis_index("az")
    g = lax.axis_index("rg")

    def fetch(src, dst, at):
        copy = pltpu.make_async_copy(src, dst, local_sem.at[at])
        copy.start()
        return copy

    echo_copy = fetch(echo_hbm, echo, 0)
    chirp_copy = fetch(chirp_hbm, chirp, 1)
    shifts_copy = fetch(shifts_hbm, shifts, 2)
    index_copy = fetch(tap_index_hbm, tap_index, 3)
    table_copy = fetch(table_hbm, table, 4)
    trig_copy = fetch(trig_hbm.at[me], trig, 5)
    filt_copy = fetch(filt_hbm, filt, 6)

    barrier = pltpu.get_barrier_semaphore()

    def greet(k, carry):
        pl.semaphore_signal(
            barrier, inc=1, device_id=(lax.rem(me + k, n), g), device_id_type=MESH
        )
        return carry

    lax.fori_loop(1, n, greet, 0)
    for d in (1, 2, ng - 2, ng - 1):
        pl.semaphore_signal(barrier, inc=1, device_id=(me, lax.rem(g + d, ng)), device_id_type=MESH)

    echo_copy.wait()
    for s in range(groups):
        at = slice(HALF * s, HALF * (s + 1))
        wide[SUB * s : SUB * (s + 1), 0:cells] = jnp.concatenate(
            [echo[0, at, :], echo[1, at, :]], axis=0
        ).astype(BF16)

    pl.semaphore_wait(barrier, n - 1 + 4)

    def halo_copy(src, dst, slot, d):
        return pltpu.make_async_remote_copy(
            src_ref=src,
            dst_ref=dst,
            send_sem=halo_send.at[slot],
            recv_sem=halo_recv.at[slot],
            device_id=(me, lax.rem(g - d + ng, ng)),
            device_id_type=MESH,
        )

    def echo_copy_of(d, h):
        return halo_copy(
            wide.at[:, pl.ds(part * h, part)],
            wide.at[:, pl.ds(d * cells + part * h, part)],
            PARTS * (d - 1) + h,
            d,
        )

    for d in (1, 2):
        for h in range(PARTS):
            pl.when(g >= d)(echo_copy_of(d, h).start)

    chirp_copy.wait()
    span = chirp_len + 2 * block
    row_id = lax.broadcasted_iota(jnp.int32, (LANE, LANE), 0)
    col_id = lax.broadcasted_iota(jnp.int32, (LANE, LANE), 1)
    mirror = (row_id + col_id == LANE - 1).astype(BF16)
    pieces = [
        jnp.dot(chirp[:, LANE * i : LANE * (i + 1)], mirror, preferred_element_type=F32)
        for i in reversed(range(chirp_len // LANE))
    ]
    edge = jnp.zeros((2, block), F32)
    base = jnp.concatenate([edge] + pieces + [edge], axis=1)
    for c in range(2):
        copies = jnp.broadcast_to(base[c : c + 1], (LANE, span))
        band[c] = pltpu.roll(copies, 1, 1, stride=1, stride_axis=0).astype(BF16)
    for a in range((chirp_len + block) // LANE):
        start = chirp_len + block - LANE * a
        for c in range(2):
            weights[LANE * a : LANE * (a + 1), block * c : block * (c + 1)] = band[
                c, :, start : start + block
            ]

    shifts_copy.wait()
    index_copy.wait()
    table_copy.wait()
    phases = table.shape[1]
    on_row = lax.broadcasted_iota(jnp.int32, (2 * rows, rows), 0)
    on_col = lax.broadcasted_iota(jnp.int32, (2 * rows, rows), 1)
    row_of = lax.div(on_row, SUB) * HALF + lax.rem(on_row, HALF)

    def across(values):
        return jnp.broadcast_to(values.astype(F32).reshape(1, rows), (2 * rows, rows))

    def pick(mask, values):
        return jnp.sum(jnp.where(mask, values, 0.0), axis=1, keepdims=True)

    shift_row = across(shifts[...])
    shift = pick(row_of == on_col, shift_row)
    distant = shift >= float(cells)
    rank = pick(on_col < row_of, jnp.where(shift_row >= float(cells), 1.0, 0.0))
    plain_row = lax.broadcasted_iota(jnp.int32, (rows, rows), 0)
    plain_col = lax.broadcasted_iota(jnp.int32, (rows, rows), 1)

    def upright(values):
        spread_out = jnp.broadcast_to(values.astype(F32).reshape(1, rows), (rows, rows))
        return pick(plain_row == plain_col, spread_out)

    shift_wide[...] = jnp.broadcast_to(upright(shifts[...]).astype(jnp.int32), (rows, LANE))
    phase_id = lax.broadcasted_iota(jnp.int32, (rows, phases), 1).astype(F32)
    coefs = lax.dot_general(
        jnp.where(upright(tap_index[...]) == phase_id, 1.0, 0.0),
        table[...],
        (((1,), (1,)), ((), ())),
        precision=lax.Precision.HIGHEST,
        preferred_element_type=F32,
    )
    for q in range(coef_wide.shape[0]):
        coef_wide[q] = jnp.broadcast_to(coefs[:, q : q + 1], (rows, LANE))
    from_row = lax.broadcasted_iota(jnp.int32, (2 * rows, 2 * slots), 0)
    to_slot = lax.broadcasted_iota(jnp.int32, (2 * rows, 2 * slots), 1)
    same_part = lax.rem(lax.div(from_row, HALF), 2) == lax.rem(lax.div(to_slot, HALF), 2)
    slot_of = (lax.div(to_slot, SUB) * HALF + lax.rem(to_slot, HALF)).astype(F32)
    matches = jnp.where(rank == slot_of, 1.0, 0.0) * jnp.where(same_part, 1.0, 0.0)
    matches = matches * jnp.where(distant, 1.0, 0.0)
    spread[...] = matches.astype(BF16)
    gathering[...] = matches.T.astype(BF16)

    def tile(ref, h, q):
        row = pl.multiple_of(SUB * lax.div(q, lanes), SUB)
        col = pl.multiple_of(LANE * lax.rem(q, lanes), LANE)
        return ref.at[h, pl.ds(row, SUB), pl.ds(col, LANE)]

    def away(i, count):
        return count // 2 + (1 - 2 * lax.rem(i, 2)) * lax.div(i + 1, 2)

    def partner(k):
        y = lax.rem(lax.div(me, nz) + away(lax.rem(k, n // nz), n // nz), n // nz)
        z = lax.rem(lax.rem(me, nz) + away(lax.div(k, n // nz), nz), nz)
        return y * nz + z

    def exchange(source, target, phase, h):
        at = PARTS * phase + h
        pltpu.make_async_copy(source(me), target(me), az_recv.at[at]).start()

        def start(k, carry):
            q = partner(k)
            pltpu.make_async_remote_copy(
                src_ref=source(q),
                dst_ref=target(me),
                send_sem=az_send.at[at],
                recv_sem=az_recv.at[at],
                device_id=(q, g),
                device_id_type=MESH,
            ).start()
            return carry

        lax.fori_loop(0, n - 1, start, 0)

    def scatter(src, dst, phase, h):
        exchange(lambda q: tile(src, h, q), lambda p: dst.at[h, p], phase, h)

    def gather(src, dst, phase, h):
        exchange(lambda q: src.at[h, q], lambda p: tile(dst, h, p), phase, h)

    def arrived(dst, phase, h):
        pltpu.make_async_copy(dst.at[h], dst.at[h], az_recv.at[PARTS * phase + h]).wait()

    def transform(fft, src, dst, h):
        xs = []
        for p in range(n):
            value = decode(src[h, p])
            xs.append((value[:HALF], value[HALF:]))
        for p, (re, im) in enumerate(fft(xs)):
            dst[h, p] = encode(jnp.concatenate([re, im], axis=0) * (1.0 / math.sqrt(n)))

    def compress(h):
        starts = range(part * h, part * (h + 1), block)
        left = jnp.concatenate([wide[:, m : m + chirp_len + block] for m in starts], axis=0)
        product = jnp.dot(left, weights[...], preferred_element_type=F32)
        for i, _ in enumerate(starts):
            piece = product[2 * rows * i : 2 * rows * (i + 1)].reshape(groups, 2, HALF, 2 * block)
            real = piece[:, 0, :, :block] - piece[:, 1, :, block:]
            imag = piece[:, 0, :, block:] + piece[:, 1, :, :block]
            both = jnp.concatenate([real, imag], axis=1).reshape(2 * rows, block)
            send_1[h, :, block * i : block * (i + 1)] = encode(both)

    def echo_arrived(d, h):
        pl.when(g + d < ng)(echo_copy_of(d, h).wait_recv)

        @pl.when(g + d >= ng)
        def _():
            start = d * cells + part * h
            wide[:, start : start + part] = jnp.zeros((2 * rows, part), BF16)

    for h in range(PARTS):
        echo_arrived(1, h)
    for h in range(PARTS):
        echo_arrived(2, h)
        compress(h)
        scatter(send_1, recv_1, 0, h)

    for h in range(PARTS):
        arrived(recv_1, 0, h)
        transform(fft_forward, recv_1, send_2, h)
        gather(send_2, recv_2, 1, h)

    def times(at, upper, lower):
        return jnp.dot(
            jnp.concatenate([trig[at], trig[at + 1], trig[at]], axis=1),
            jnp.concatenate([upper, upper, lower], axis=0),
            preferred_element_type=F32,
        )

    def split(value):
        upper = value.astype(BF16)
        return upper, (value - upper.astype(F32)).astype(BF16)

    def spec_copy_of(d, h):
        src, dst = ((spec_code, halo_1), (far_code, halo_2))[d - 1]
        return halo_copy(src.at[h], dst.at[h], 2 * PARTS + PARTS * (d - 1) + h, d)

    trig_copy.wait()
    for h in range(PARTS):
        arrived(recv_2, 1, h)
        spectrum = times(0, *split(decode(recv_2[h])))
        code = encode(spectrum)
        spec_code[h] = code
        pl.when(g >= 1)(spec_copy_of(1, h).start)
        far_code[h] = jnp.dot(gathering[...], code, preferred_element_type=F32).astype(BF16)
        pl.when(g >= 2)(spec_copy_of(2, h).start)
        spec[:, part * h : part * (h + 1)] = spectrum

    def spec_arrived(d, h):
        dst = (halo_1, halo_2)[d - 1]
        pl.when(g + d < ng)(spec_copy_of(d, h).wait_recv)

        @pl.when(g + d >= ng)
        def _():
            dst[h] = jnp.zeros(dst.shape[1:], BF16)

        start = d * cells + part * h
        if d == 1:
            value = halo_1[h]
        else:
            value = jnp.dot(spread[...], halo_2[h], preferred_element_type=F32)
        spec[:, start : start + part] = decode(value)

    taps = coef_wide.shape[0]

    lane = lax.broadcasted_iota(jnp.int32, (HALF, LANE), 1)
    block_tiles = cells // LANE

    def migrate(h):
        start = part * h

        def row_group(j):
            at = pl.multiple_of(SUB * j, SUB)
            own = pl.multiple_of(HALF * j, HALF)
            shift = shift_wide[pl.ds(own, HALF), :]
            distant = shift >= cells
            rest = jnp.where(distant, shift - cells, shift)
            fine = rest & (LANE - 1)
            turned = lane + fine
            inside = turned < LANE
            turned = jnp.where(inside, turned, turned - LANE)
            totals = []
            for c in range(2):
                row = pl.ds(pl.multiple_of(at + HALF * c, HALF), HALF)

                def load(t):
                    return spec[row, start + LANE * t : start + LANE * (t + 1)]

                count = lanes + block_tiles
                cur = [
                    jnp.where(distant, load(t + block_tiles), load(t)) for t in range(count)
                ]
                step = block_tiles // 2
                while step >= 1:
                    bit = (rest & (step * LANE)) != 0
                    width = lanes + step + 1
                    cur = [
                        jnp.where(bit, cur[min(t + step, count - 1)], cur[t]) for t in range(width)
                    ]
                    count = width
                    step //= 2
                cur = [jnp.take_along_axis(x, turned, axis=1) for x in cur]
                cur = [jnp.where(inside, cur[t], cur[t + 1]) for t in range(lanes + 1)]
                total = [coef_wide[0, pl.ds(own, HALF), :] * cur[t] for t in range(lanes)]
                for q in range(1, taps):
                    weight = coef_wide[q, pl.ds(own, HALF), :]
                    moved = [pltpu.roll(x, LANE - q, 1) for x in cur]
                    kept = lane < LANE - q
                    total = [
                        total[t] + weight * jnp.where(kept, moved[t], moved[t + 1])
                        for t in range(lanes)
                    ]
                totals.append(total)
            for t in range(lanes):
                col = slice(LANE * t, LANE * (t + 1))
                fr = filt[0, pl.ds(own, HALF), start + LANE * t : start + LANE * (t + 1)]
                fi = filt[1, pl.ds(own, HALF), start + LANE * t : start + LANE * (t + 1)]
                x, y = totals[0][t], totals[1][t]
                both = jnp.concatenate([x * fr - y * fi, x * fi + y * fr], axis=0)
                upper, lower = split(both)
                high[h, pl.ds(at, SUB), col] = upper
                low[h, pl.ds(at, SUB), col] = lower

        def some(j, carry):
            for u in range(UNROLL):
                row_group(UNROLL * j + u)
            return carry

        lax.fori_loop(0, groups // UNROLL, some, 0)

    spec_arrived(1, 0)
    spec_arrived(2, 0)
    spec_arrived(1, 1)
    filt_copy.wait()
    for h in range(PARTS):
        if h == PARTS - 1:
            spec_arrived(2, h)
        migrate(h)
        send_3[h] = encode(times(2, high[h], low[h]))
        scatter(send_3, recv_3, 2, h)

    for h in range(PARTS):
        arrived(recv_3, 2, h)
        transform(fft_inverse, recv_3, send_4, h)
        gather(send_4, recv_4, 3, h)
    for h in range(PARTS):
        arrived(recv_4, 3, h)
        for s in range(groups):
            value = decode(recv_4[h, SUB * s : SUB * (s + 1), :])
            for c in range(2):
                out[c, HALF * s : HALF * (s + 1), part * h : part * (h + 1)] = value[
                    HALF * c : HALF * (c + 1)
                ]

    for d in (1, 2):
        for h in range(PARTS):
            pl.when(g >= d)(echo_copy_of(d, h).wait_send)
            pl.when(g >= d)(spec_copy_of(d, h).wait_send)
    for at in range(4 * PARTS):
        sent = send_2.at[0, pl.ds(0, n - 1)]
        pltpu.make_async_copy(sent, sent, az_send.at[at]).wait()


def solution(mesh):
    n, ng = mesh.shape["az"], mesh.shape["rg"]

    def local(echo_field, range_chirp, azimuth_filter, shifts, tap_index, taps_table):
        rows, cells = echo_field.shape[1], echo_field.shape[2]
        chirp_len = range_chirp.shape[1]
        phases, taps = taps_table.shape
        block = 256
        slots = rows // 2
        part = cells // PARTS
        trig = jnp.asarray(trig_tables(n, rows))
        stack = (2, rows, cells)
        flat = (PARTS, 2 * rows, part)
        tiles = (PARTS, n, SUB, LANE)
        hbm = pl.BlockSpec(memory_space=pltpu.HBM)
        return pl.pallas_call(
            functools.partial(kernel, n, ng, slots),
            out_shape=jax.ShapeDtypeStruct(stack, F32),
            in_specs=[hbm] * 7,
            out_specs=pl.BlockSpec(memory_space=pltpu.VMEM),
            scratch_shapes=[
                pltpu.VMEM(stack, F32),
                pltpu.VMEM((2, chirp_len), BF16),
                pltpu.VMEM(stack, F32),
                pltpu.VMEM((rows,), jnp.int32),
                pltpu.VMEM((rows,), jnp.int32),
                pltpu.VMEM((taps, phases), F32),
                pltpu.VMEM((4, 2 * rows, 2 * rows), BF16),
                pltpu.VMEM((2, LANE, chirp_len + 2 * block), BF16),
                pltpu.VMEM((chirp_len + block, 2 * block), BF16),
                pltpu.VMEM((2 * rows, 3 * cells), BF16),
                pltpu.VMEM((rows, LANE), jnp.int32),
                pltpu.VMEM((taps, rows, LANE), F32),
                pltpu.VMEM((2 * rows, 2 * slots), BF16),
                pltpu.VMEM((2 * slots, 2 * rows), BF16),
                pltpu.VMEM(flat, BF16),
                pltpu.VMEM(tiles, BF16),
                pltpu.VMEM(tiles, BF16),
                pltpu.VMEM(flat, BF16),
                pltpu.VMEM((2 * rows, 3 * cells), F32),
                pltpu.VMEM(flat, BF16),
                pltpu.VMEM((PARTS, 2 * slots, part), BF16),
                pltpu.VMEM(flat, BF16),
                pltpu.VMEM((PARTS, 2 * slots, part), BF16),
                pltpu.VMEM(flat, BF16),
                pltpu.VMEM(flat, BF16),
                pltpu.VMEM(flat, BF16),
                pltpu.VMEM(tiles, BF16),
                pltpu.VMEM(tiles, BF16),
                pltpu.VMEM(flat, BF16),
                pltpu.SemaphoreType.DMA((7,)),
                pltpu.SemaphoreType.DMA((4 * PARTS,)),
                pltpu.SemaphoreType.DMA((4 * PARTS,)),
                pltpu.SemaphoreType.DMA((4 * PARTS,)),
                pltpu.SemaphoreType.DMA((4 * PARTS,)),
            ],
            compiler_params=pltpu.CompilerParams(
                collective_id=0, has_side_effects=True, vmem_limit_bytes=62 * 1024 * 1024
            ),
            cost_estimate=pl.CostEstimate(
                flops=1_600_000_000, bytes_accessed=2_000_000, transcendentals=0
            ),
        )(echo_field, range_chirp, azimuth_filter, shifts, tap_index, taps_table.T, trig)

    placed = (P(None, "az", "rg"), P(), P(None, "az", "rg"), P("az"), P("az"), P())
    return jax.shard_map(
        local, mesh=mesh, in_specs=placed, out_specs=P(None, "az", "rg"), check_vma=False
    )
```

```python
import functools
import math

import jax
import jax.numpy as jnp
import numpy as np
from jax import lax
from jax.experimental import pallas as pl
from jax.experimental.pallas import tpu as pltpu
from jax.sharding import PartitionSpec as P

MESH = pl.DeviceIdType.MESH
F32 = jnp.float32
BF16 = jnp.bfloat16
LANE = 128
SUB = 16
HALF = 8
PARTS = 4
JOBS = 2
PASSED = 3
UNROLL = 4


def encode(x):
    return (x * jnp.abs(x)).astype(BF16)


def decode(code):
    c = code.astype(F32)
    return c * lax.rsqrt(jnp.maximum(jnp.abs(c), 1e-37))


def bit_reverse(value, bits):
    result = 0
    for position in range(bits):
        result += ((value >> position) & 1) << (bits - 1 - position)
    return result


def turn(pair, k, n, sign):
    re, im = pair
    if k == 0:
        return re, im
    if 4 * k == n:
        return (-im, re) if sign > 0 else (im, -re)
    c = math.cos(2 * math.pi * k / n)
    s = sign * math.sin(2 * math.pi * k / n)
    if 8 * k == n:
        return ((re - im) * c, (re + im) * c) if sign > 0 else ((re + im) * c, (im - re) * c)
    if 8 * k == 3 * n:
        h = -c
        return (-(re + im) * h, (re - im) * h) if sign > 0 else ((im - re) * h, -(re + im) * h)
    return re * c - im * s, re * s + im * c


def fft_forward(xs):
    n = len(xs)
    if n == 1:
        return xs
    half = n // 2
    low, high = [], []
    for k in range(half):
        (ar, ai), (br, bi) = xs[k], xs[k + half]
        low.append((ar + br, ai + bi))
        high.append(turn((ar - br, ai - bi), k, n, -1))
    return fft_forward(low) + fft_forward(high)


def fft_inverse(xs):
    n = len(xs)
    if n == 1:
        return xs
    half = n // 2
    low = fft_inverse(xs[:half])
    high = fft_inverse(xs[half:])
    first, second = [], []
    for k in range(half):
        ar, ai = low[k]
        br, bi = turn(high[k], k, n, 1)
        first.append((ar + br, ai + bi))
        second.append((ar - br, ai - bi))
    return first + second


def packed(rows):
    group, part, inner = np.meshgrid(
        np.arange(rows // HALF), np.arange(2), np.arange(HALF), indexing="ij"
    )
    return (part * rows + group * HALF + inner).reshape(-1)


def trig_tables(n_az, rows):
    total = n_az * rows
    bits = n_az.bit_length() - 1
    order = packed(rows)
    tables = np.zeros((n_az, 4, 2 * rows, 2 * rows), np.float32)
    s = np.arange(rows)[None, :]
    j = np.arange(rows)[:, None]
    for p in range(n_az):
        b = bit_reverse(p, bits)
        angle = 2 * np.pi * ((s * (b + n_az * j)) % total) / total
        c, d = np.cos(angle) / math.sqrt(rows), np.sin(angle) / math.sqrt(rows)
        m = np.block([[c, d], [-d, c]])[np.ix_(order, order)]
        for at, mat in ((0, m), (2, m.T)):
            high = mat.astype(np.float32).astype(jnp.bfloat16)
            tables[p, at] = high.astype(np.float32)
            tables[p, at + 1] = mat - high.astype(np.float64)
    return tables.astype(jnp.bfloat16)


def kernel(
    n,
    ng,
    slots,
    echo_hbm,
    chirp_hbm,
    filt_hbm,
    shifts_hbm,
    tap_index_hbm,
    table_hbm,
    trig_hbm,
    out,
    echo,
    chirp,
    filt,
    shifts,
    tap_index,
    table,
    trig,
    band,
    weights,
    wide,
    shift_wide,
    coef_wide,
    spread,
    gathering,
    send_1,
    recv_1,
    send_2,
    recv_2,
    spec,
    spec_code,
    far_code,
    halo_1,
    halo_2,
    high,
    low,
    send_3,
    recv_3,
    send_4,
    recv_4,
    local_sem,
    halo_send,
    halo_recv,
    pass_send,
    part_send,
    part_recv,
    job_send,
    job_recv,
):
    rows, cells = echo.shape[1], echo.shape[2]
    chirp_len = chirp.shape[1]
    part = cells // PARTS
    lanes = part // LANE
    groups = rows // HALF
    block = 256
    nz = 8
    me = lax.axis_index("az")
    g = lax.axis_index("rg")

    def fetch(src, dst, at):
        copy = pltpu.make_async_copy(src, dst, local_sem.at[at])
        copy.start()
        return copy

    echo_copy = fetch(echo_hbm, echo, 0)
    chirp_copy = fetch(chirp_hbm, chirp, 1)
    shifts_copy = fetch(shifts_hbm, shifts, 2)
    index_copy = fetch(tap_index_hbm, tap_index, 3)
    table_copy = fetch(table_hbm, table, 4)
    trig_copy = fetch(trig_hbm.at[me], trig, 5)
    filt_copy = fetch(filt_hbm, filt, 6)

    barrier = pltpu.get_barrier_semaphore()

    def greet(k, carry):
        pl.semaphore_signal(
            barrier, inc=1, device_id=(lax.rem(me + k, n), g), device_id_type=MESH
        )
        return carry

    lax.fori_loop(1, n, greet, 0)
    for d in (1, 2, ng - 2, ng - 1):
        pl.semaphore_signal(barrier, inc=1, device_id=(me, lax.rem(g + d, ng)), device_id_type=MESH)

    echo_copy.wait()
    for s in range(groups):
        at = slice(HALF * s, HALF * (s + 1))
        wide[SUB * s : SUB * (s + 1), 0:cells] = jnp.concatenate(
            [echo[0, at, :], echo[1, at, :]], axis=0
        ).astype(BF16)

    pl.semaphore_wait(barrier, n - 1 + 4)

    def halo_copy(src, dst, slot, d):
        return pltpu.make_async_remote_copy(
            src_ref=src,
            dst_ref=dst,
            send_sem=halo_send.at[slot],
            recv_sem=halo_recv.at[slot],
            device_id=(me, lax.rem(g - d + ng, ng)),
            device_id_type=MESH,
        )

    odd = lax.rem(g, 2) == 1

    def sends_echo(d, h):
        far_enough = g >= d
        return far_enough & odd if d == 2 and h < PASSED else far_enough

    def pass_on(h):
        return pltpu.make_async_remote_copy(
            src_ref=wide.at[:, pl.ds(cells + part * h, part)],
            dst_ref=wide.at[:, pl.ds(2 * cells + part * h, part)],
            send_sem=pass_send.at[h],
            recv_sem=halo_recv.at[PARTS + h],
            device_id=(me, lax.rem(g - 1 + ng, ng)),
            device_id_type=MESH,
        )

    passes_on = odd & (g + 1 < ng)

    def echo_copy_of(d, h):
        return halo_copy(
            wide.at[:, pl.ds(part * h, part)],
            wide.at[:, pl.ds(d * cells + part * h, part)],
            PARTS * (d - 1) + h,
            d,
        )

    for d in (1, 2):
        for h in range(PARTS):
            pl.when(sends_echo(d, h))(echo_copy_of(d, h).start)

    chirp_copy.wait()
    span = chirp_len + 2 * block
    row_id = lax.broadcasted_iota(jnp.int32, (LANE, LANE), 0)
    col_id = lax.broadcasted_iota(jnp.int32, (LANE, LANE), 1)
    mirror = (row_id + col_id == LANE - 1).astype(BF16)
    pieces = [
        jnp.dot(chirp[:, LANE * i : LANE * (i + 1)], mirror, preferred_element_type=F32)
        for i in reversed(range(chirp_len // LANE))
    ]
    edge = jnp.zeros((2, block), F32)
    base = jnp.concatenate([edge] + pieces + [edge], axis=1)
    for c in range(2):
        copies = jnp.broadcast_to(base[c : c + 1], (LANE, span))
        band[c] = pltpu.roll(copies, 1, 1, stride=1, stride_axis=0).astype(BF16)
    for a in range((chirp_len + block) // LANE):
        start = chirp_len + block - LANE * a
        for c in range(2):
            weights[LANE * a : LANE * (a + 1), block * c : block * (c + 1)] = band[
                c, :, start : start + block
            ]

    shifts_copy.wait()
    index_copy.wait()
    table_copy.wait()
    phases = table.shape[1]
    on_row = lax.broadcasted_iota(jnp.int32, (2 * rows, rows), 0)
    on_col = lax.broadcasted_iota(jnp.int32, (2 * rows, rows), 1)
    row_of = lax.div(on_row, SUB) * HALF + lax.rem(on_row, HALF)

    def across(values):
        return jnp.broadcast_to(values.astype(F32).reshape(1, rows), (2 * rows, rows))

    def pick(mask, values):
        return jnp.sum(jnp.where(mask, values, 0.0), axis=1, keepdims=True)

    shift_row = across(shifts[...])
    shift = pick(row_of == on_col, shift_row)
    distant = shift >= float(cells)
    rank = pick(on_col < row_of, jnp.where(shift_row >= float(cells), 1.0, 0.0))
    plain_row = lax.broadcasted_iota(jnp.int32, (rows, rows), 0)
    plain_col = lax.broadcasted_iota(jnp.int32, (rows, rows), 1)

    def upright(values):
        spread_out = jnp.broadcast_to(values.astype(F32).reshape(1, rows), (rows, rows))
        return pick(plain_row == plain_col, spread_out)

    shift_wide[...] = jnp.broadcast_to(upright(shifts[...]).astype(jnp.int32), (rows, LANE))
    phase_id = lax.broadcasted_iota(jnp.int32, (rows, phases), 1).astype(F32)
    coefs = lax.dot_general(
        jnp.where(upright(tap_index[...]) == phase_id, 1.0, 0.0),
        table[...],
        (((1,), (1,)), ((), ())),
        precision=lax.Precision.HIGHEST,
        preferred_element_type=F32,
    )
    for q in range(coef_wide.shape[0]):
        coef_wide[q] = jnp.broadcast_to(coefs[:, q : q + 1], (rows, LANE))
    from_row = lax.broadcasted_iota(jnp.int32, (2 * rows, 2 * slots), 0)
    to_slot = lax.broadcasted_iota(jnp.int32, (2 * rows, 2 * slots), 1)
    same_part = lax.rem(lax.div(from_row, HALF), 2) == lax.rem(lax.div(to_slot, HALF), 2)
    slot_of = (lax.div(to_slot, SUB) * HALF + lax.rem(to_slot, HALF)).astype(F32)
    matches = jnp.where(rank == slot_of, 1.0, 0.0) * jnp.where(same_part, 1.0, 0.0)
    matches = matches * jnp.where(distant, 1.0, 0.0)
    spread[...] = matches.astype(BF16)
    gathering[...] = matches.T.astype(BF16)

    ny = n // nz
    my_y, my_z = lax.div(me, nz), lax.rem(me, nz)
    parity = lax.rem(me, 2)
    spot = my_y * (nz // 2) + lax.div(my_z, 2)

    def away(i, count):
        return count // 2 + (1 - 2 * lax.rem(i, 2)) * lax.div(i + 1, 2)

    def tile(ref, p, at):
        row = pl.multiple_of(SUB * lax.div(at, lanes), SUB)
        col = pl.multiple_of(LANE * lax.rem(at, lanes), LANE)
        return ref.at[p, pl.ds(row, SUB), pl.ds(col, LANE)]

    def other(p):
        return lax.rem(parity + p, 2)

    def scatter(src, dst, phase, p):
        job = p // JOBS

        def start(k, carry):
            y = lax.rem(my_y + away(lax.rem(k, ny), ny), ny)
            z = lax.rem(my_z + 2 * away(lax.div(k, ny), nz // 2) + other(p), nz)
            pltpu.make_async_remote_copy(
                src_ref=tile(src, p, y * (nz // 2) + lax.div(z, 2)),
                dst_ref=dst.at[job, me],
                send_sem=part_send.at[phase, p],
                recv_sem=job_recv.at[phase, job],
                device_id=(y * nz + z, g),
                device_id_type=MESH,
            ).start()
            return carry

        lax.fori_loop(0, n // 2 - 1 + other(p), start, 0)

        @pl.when(other(p) == 0)
        def _():
            pltpu.make_async_copy(
                tile(src, p, spot), dst.at[job, me], job_recv.at[phase, job]
            ).start()

    def gather(src, dst, phase, job):
        p = 2 * job + parity

        def start(k, carry):
            y = lax.rem(my_y + away(lax.rem(k, ny), ny), ny)
            z = lax.rem(my_z + away(lax.div(k, ny), nz), nz)
            q = y * nz + z
            pltpu.make_async_remote_copy(
                src_ref=src.at[job, q],
                dst_ref=tile(dst, p, spot),
                send_sem=job_send.at[phase, job],
                recv_sem=part_recv.at[phase, p],
                device_id=(q, g),
                device_id_type=MESH,
            ).start()
            return carry

        lax.fori_loop(0, n - 1, start, 0)
        pltpu.make_async_copy(src.at[job, me], tile(dst, p, spot), part_recv.at[phase, p]).start()

    def scattered(dst, phase, job):
        pltpu.make_async_copy(dst.at[job], dst.at[job], job_recv.at[phase, job]).wait()

    def gathered(dst, phase, p):
        pltpu.make_async_copy(dst.at[p], dst.at[p], part_recv.at[phase, p]).wait()

    def transform(fft, src, dst, h):
        xs = []
        for p in range(n):
            value = decode(src[h, p])
            xs.append((value[:HALF], value[HALF:]))
        for p, (re, im) in enumerate(fft(xs)):
            dst[h, p] = encode(jnp.concatenate([re, im], axis=0) * (1.0 / math.sqrt(n)))

    def compress(h):
        left = wide[:, part * h : part * h + chirp_len + block]
        product = jnp.dot(left, weights[...], preferred_element_type=F32)
        piece = product.reshape(groups, 2, HALF, 2 * block)
        real = piece[:, 0, :, :block] - piece[:, 1, :, block:]
        imag = piece[:, 0, :, block:] + piece[:, 1, :, :block]
        send_1[h] = encode(jnp.concatenate([real, imag], axis=1).reshape(2 * rows, block))

    def echo_arrived(d, h):
        pl.when(g + d < ng)(echo_copy_of(d, h).wait_recv)

        @pl.when(g + d >= ng)
        def _():
            start = d * cells + part * h
            wide[:, start : start + part] = jnp.zeros((2 * rows, part), BF16)

    for h in range(PARTS):
        echo_arrived(1, h)
        if h < PASSED:
            pl.when(passes_on)(pass_on(h).start)
    for h in range(PARTS):
        echo_arrived(2, h)
        compress(h)
        scatter(send_1, recv_1, 0, h)

    for job in range(JOBS):
        scattered(recv_1, 0, job)
        transform(fft_forward, recv_1, send_2, job)
        gather(send_2, recv_2, 0, job)

    def times(at, upper, lower):
        return jnp.dot(
            jnp.concatenate([trig[at], trig[at + 1], trig[at]], axis=1),
            jnp.concatenate([upper, upper, lower], axis=0),
            preferred_element_type=F32,
        )

    def split(value):
        upper = value.astype(BF16)
        return upper, (value - upper.astype(F32)).astype(BF16)

    def spec_copy_of(d, h):
        src, dst = ((spec_code, halo_1), (far_code, halo_2))[d - 1]
        return halo_copy(src.at[h], dst.at[h], 2 * PARTS + PARTS * (d - 1) + h, d)

    trig_copy.wait()
    for h in range(PARTS):
        gathered(recv_2, 0, h)
        spectrum = times(0, *split(decode(recv_2[h])))
        code = encode(spectrum)
        spec_code[h] = code
        pl.when(g >= 1)(spec_copy_of(1, h).start)
        far_code[h] = jnp.dot(gathering[...], code, preferred_element_type=F32).astype(BF16)
        pl.when(g >= 2)(spec_copy_of(2, h).start)
        spec[:, part * h : part * (h + 1)] = spectrum

    def spec_arrived(d, h):
        dst = (halo_1, halo_2)[d - 1]
        pl.when(g + d < ng)(spec_copy_of(d, h).wait_recv)

        @pl.when(g + d >= ng)
        def _():
            dst[h] = jnp.zeros(dst.shape[1:], BF16)

        start = d * cells + part * h
        if d == 1:
            value = halo_1[h]
        else:
            value = jnp.dot(spread[...], halo_2[h], preferred_element_type=F32)
        spec[:, start : start + part] = decode(value)


    lane = lax.broadcasted_iota(jnp.int32, (HALF, LANE), 1)
    block_tiles = cells // LANE
    reach = cells // 2
    lanes_out = reach // LANE

    def ahead(xs, by):
        moved = [pltpu.roll(x, LANE - by, 1) for x in xs]
        kept = lane < LANE - by
        return [jnp.where(kept, a, b) for a, b in zip(moved, moved[1:])] + [moved[-1]]

    def migrate(h):
        start = reach * h

        def row_group(j):
            at = pl.multiple_of(SUB * j, SUB)
            own = pl.multiple_of(HALF * j, HALF)
            shift = shift_wide[pl.ds(own, HALF), :]
            distant = shift >= cells
            rest = jnp.where(distant, shift - cells, shift)
            fine = rest & (LANE - 1)
            turned = lane + fine
            inside = turned < LANE
            turned = jnp.where(inside, turned, turned - LANE)
            totals = []
            for c in range(2):
                row = pl.ds(pl.multiple_of(at + HALF * c, HALF), HALF)

                def load(t):
                    return spec[row, start + LANE * t : start + LANE * (t + 1)]

                count = lanes_out + block_tiles
                cur = [
                    jnp.where(distant, load(t + block_tiles), load(t)) for t in range(count)
                ]
                step = block_tiles // 2
                while step >= 1:
                    bit = (rest & (step * LANE)) != 0
                    width = lanes_out + step + 1
                    cur = [
                        jnp.where(bit, cur[min(t + step, count - 1)], cur[t]) for t in range(width)
                    ]
                    count = width
                    step //= 2
                cur = [jnp.take_along_axis(x, turned, axis=1) for x in cur]
                cur = [jnp.where(inside, cur[t], cur[t + 1]) for t in range(lanes_out + 1)]
                weight = [coef_wide[q, pl.ds(own, HALF), :] for q in range(8)]
                four = ahead(cur, 4)
                pair = [
                    [weight[q] * x + weight[q + 4] * y for x, y in zip(cur, four)]
                    for q in range(4)
                ]
                even = [x + y for x, y in zip(pair[0], ahead(pair[2], 2))]
                odd = [x + y for x, y in zip(pair[1], ahead(pair[3], 2))]
                total = [x + y for x, y in zip(even, ahead(odd, 1))]
                totals.append(total)
            for t in range(lanes_out):
                col = slice(start + LANE * t, start + LANE * (t + 1))
                fr = filt[0, pl.ds(own, HALF), col]
                fi = filt[1, pl.ds(own, HALF), col]
                x, y = totals[0][t], totals[1][t]
                both = jnp.concatenate([x * fr - y * fi, x * fi + y * fr], axis=0)
                upper, lower = split(both)
                high[pl.ds(at, SUB), col] = upper
                low[pl.ds(at, SUB), col] = lower

        def some(j, carry):
            for u in range(UNROLL):
                row_group(UNROLL * j + u)
            return carry

        lax.fori_loop(0, groups // UNROLL, some, 0)

    for h in range(PARTS):
        spec_arrived(1, h)
    filt_copy.wait()
    for half in range(2):
        for h in range(PARTS // 2 * half, PARTS // 2 * (half + 1)):
            spec_arrived(2, h)
        migrate(half)
        for h in range(PARTS // 2 * half, PARTS // 2 * (half + 1)):
            col = slice(part * h, part * (h + 1))
            send_3[h] = encode(times(2, high[:, col], low[:, col]))
            scatter(send_3, recv_3, 1, h)

    for job in range(JOBS):
        scattered(recv_3, 1, job)
        transform(fft_inverse, recv_3, send_4, job)
        gather(send_4, recv_4, 1, job)
    for h in range(PARTS):
        gathered(recv_4, 1, h)
        for s in range(groups):
            value = decode(recv_4[h, SUB * s : SUB * (s + 1), :])
            for c in range(2):
                out[c, HALF * s : HALF * (s + 1), part * h : part * (h + 1)] = value[
                    HALF * c : HALF * (c + 1)
                ]

    for h in range(PASSED):
        pl.when(passes_on)(pass_on(h).wait_send)
    for d in (1, 2):
        for h in range(PARTS):
            pl.when(sends_echo(d, h))(echo_copy_of(d, h).wait_send)
            pl.when(g >= d)(spec_copy_of(d, h).wait_send)
    for phase in range(2):
        for job in range(JOBS):
            sent = send_2.at[0, pl.ds(0, n - 1)]
            pltpu.make_async_copy(sent, sent, job_send.at[phase, job]).wait()
        for p in range(PARTS):
            for same in (0, 1):
                sent = send_2.at[0, pl.ds(0, n // 2 - 1 + same)]
                pl.when(other(p) == same)(
                    pltpu.make_async_copy(sent, sent, part_send.at[phase, p]).wait
                )


def solution(mesh):
    n, ng = mesh.shape["az"], mesh.shape["rg"]

    def local(echo_field, range_chirp, azimuth_filter, shifts, tap_index, taps_table):
        rows, cells = echo_field.shape[1], echo_field.shape[2]
        chirp_len = range_chirp.shape[1]
        phases, taps = taps_table.shape
        block = 256
        slots = rows // 2
        part = cells // PARTS
        trig = jnp.asarray(trig_tables(n, rows))
        stack = (2, rows, cells)
        flat = (PARTS, 2 * rows, part)
        tiles = (JOBS, n, SUB, LANE)
        hbm = pl.BlockSpec(memory_space=pltpu.HBM)
        return pl.pallas_call(
            functools.partial(kernel, n, ng, slots),
            out_shape=pltpu.VMEM(stack, F32),
            in_specs=[hbm] * 7,
            out_specs=pl.BlockSpec(memory_space=pltpu.VMEM),
            scratch_shapes=[
                pltpu.VMEM(stack, F32),
                pltpu.VMEM((2, chirp_len), BF16),
                pltpu.VMEM(stack, F32),
                pltpu.VMEM((rows,), jnp.int32),
                pltpu.VMEM((rows,), jnp.int32),
                pltpu.VMEM((taps, phases), F32),
                pltpu.VMEM((4, 2 * rows, 2 * rows), BF16),
                pltpu.VMEM((2, LANE, chirp_len + 2 * block), BF16),
                pltpu.VMEM((chirp_len + block, 2 * block), BF16),
                pltpu.VMEM((2 * rows, 3 * cells), BF16),
                pltpu.VMEM((rows, LANE), jnp.int32),
                pltpu.VMEM((taps, rows, LANE), F32),
                pltpu.VMEM((2 * rows, 2 * slots), BF16),
                pltpu.VMEM((2 * slots, 2 * rows), BF16),
                pltpu.VMEM(flat, BF16),
                pltpu.VMEM(tiles, BF16),
                pltpu.VMEM(tiles, BF16),
                pltpu.VMEM(flat, BF16),
                pltpu.VMEM((2 * rows, 3 * cells), F32),
                pltpu.VMEM(flat, BF16),
                pltpu.VMEM((PARTS, 2 * slots, part), BF16),
                pltpu.VMEM(flat, BF16),
                pltpu.VMEM((PARTS, 2 * slots, part), BF16),
                pltpu.VMEM((2 * rows, cells), BF16),
                pltpu.VMEM((2 * rows, cells), BF16),
                pltpu.VMEM(flat, BF16),
                pltpu.VMEM(tiles, BF16),
                pltpu.VMEM(tiles, BF16),
                pltpu.VMEM(flat, BF16),
                pltpu.SemaphoreType.DMA((7,)),
                pltpu.SemaphoreType.DMA((4 * PARTS,)),
                pltpu.SemaphoreType.DMA((4 * PARTS,)),
                pltpu.SemaphoreType.DMA((PASSED,)),
                pltpu.SemaphoreType.DMA((2, PARTS)),
                pltpu.SemaphoreType.DMA((2, PARTS)),
                pltpu.SemaphoreType.DMA((2, JOBS)),
                pltpu.SemaphoreType.DMA((2, JOBS)),
            ],
            compiler_params=pltpu.CompilerParams(
                collective_id=0, has_side_effects=True, vmem_limit_bytes=48 * 1024 * 1024
            ),
            cost_estimate=pl.CostEstimate(
                flops=1_600_000_000, bytes_accessed=2_000_000, transcendentals=0
            ),
        )(
            *(
                pltpu.with_memory_space_constraint(x, pltpu.HBM)
                for x in (
                    echo_field,
                    range_chirp,
                    azimuth_filter,
                    shifts,
                    tap_index,
                    taps_table.T,
                    trig,
                )
            )
        )

    placed = (P(None, "az", "rg"), P(), P(None, "az", "rg"), P("az"), P("az"), P())
    return jax.shard_map(
        local, mesh=mesh, in_specs=placed, out_specs=P(None, "az", "rg"), check_vma=False
    )
```

```python
import functools
import math

import jax
import jax.numpy as jnp
import numpy as np
from jax import lax
from jax.experimental import pallas as pl
from jax.experimental.pallas import tpu as pltpu
from jax.sharding import PartitionSpec as P

MESH = pl.DeviceIdType.MESH
F32 = jnp.float32
BF16 = jnp.bfloat16
LANE = 128
SUB = 16
HALF = 8
PARTS = 4
JOBS = 2
PASSED = 3
UNROLL = 4


def encode(x):
    return (x * jnp.abs(x)).astype(BF16)


def decode(code):
    c = code.astype(F32)
    return c * lax.rsqrt(jnp.maximum(jnp.abs(c), 1e-37))


def bit_reverse(value, bits):
    result = 0
    for position in range(bits):
        result += ((value >> position) & 1) << (bits - 1 - position)
    return result


def turn(pair, k, n, sign):
    re, im = pair
    if k == 0:
        return re, im
    if 4 * k == n:
        return (-im, re) if sign > 0 else (im, -re)
    c = math.cos(2 * math.pi * k / n)
    s = sign * math.sin(2 * math.pi * k / n)
    if 8 * k == n:
        return ((re - im) * c, (re + im) * c) if sign > 0 else ((re + im) * c, (im - re) * c)
    if 8 * k == 3 * n:
        h = -c
        return (-(re + im) * h, (re - im) * h) if sign > 0 else ((im - re) * h, -(re + im) * h)
    return re * c - im * s, re * s + im * c


def fft_forward(xs):
    n = len(xs)
    if n == 1:
        return xs
    half = n // 2
    low, high = [], []
    for k in range(half):
        (ar, ai), (br, bi) = xs[k], xs[k + half]
        low.append((ar + br, ai + bi))
        high.append(turn((ar - br, ai - bi), k, n, -1))
    return fft_forward(low) + fft_forward(high)


def fft_inverse(xs):
    n = len(xs)
    if n == 1:
        return xs
    half = n // 2
    low = fft_inverse(xs[:half])
    high = fft_inverse(xs[half:])
    first, second = [], []
    for k in range(half):
        ar, ai = low[k]
        br, bi = turn(high[k], k, n, 1)
        first.append((ar + br, ai + bi))
        second.append((ar - br, ai - bi))
    return first + second


def packed(rows):
    group, part, inner = np.meshgrid(
        np.arange(rows // HALF), np.arange(2), np.arange(HALF), indexing="ij"
    )
    return (part * rows + group * HALF + inner).reshape(-1)


def trig_tables(n_az, rows):
    total = n_az * rows
    bits = n_az.bit_length() - 1
    order = packed(rows)
    tables = np.zeros((n_az, 4, 2 * rows, 2 * rows), np.float32)
    s = np.arange(rows)[None, :]
    j = np.arange(rows)[:, None]
    for p in range(n_az):
        b = bit_reverse(p, bits)
        angle = 2 * np.pi * ((s * (b + n_az * j)) % total) / total
        c, d = np.cos(angle) / math.sqrt(rows), np.sin(angle) / math.sqrt(rows)
        m = np.block([[c, d], [-d, c]])[np.ix_(order, order)]
        for at, mat in ((0, m), (2, m.T)):
            high = mat.astype(np.float32).astype(jnp.bfloat16)
            tables[p, at] = high.astype(np.float32)
            tables[p, at + 1] = mat - high.astype(np.float64)
    return tables.astype(jnp.bfloat16)


def kernel(
    n,
    ng,
    slots,
    echo_hbm,
    chirp_hbm,
    filt_hbm,
    shifts_hbm,
    tap_index_hbm,
    table_hbm,
    trig_hbm,
    out,
    echo,
    chirp,
    filt,
    shifts,
    tap_index,
    table,
    trig,
    band,
    weights,
    wide,
    partial,
    shift_wide,
    coef_wide,
    spread,
    gathering,
    send_1,
    recv_1,
    send_2,
    recv_2,
    spec,
    spec_code,
    far_code,
    halo_1,
    halo_2,
    high,
    low,
    send_3,
    recv_3,
    send_4,
    recv_4,
    local_sem,
    halo_send,
    halo_recv,
    pass_send,
    part_send,
    part_recv,
    job_send,
    job_recv,
):
    rows, cells = filt.shape[1], filt.shape[2]
    chirp_len = chirp.shape[1]
    part = cells // PARTS
    lanes = part // LANE
    groups = rows // HALF
    block = 256
    nz = 8
    me = lax.axis_index("az")
    g = lax.axis_index("rg")

    def fetch(src, dst, at):
        copy = pltpu.make_async_copy(src, dst, local_sem.at[at])
        copy.start()
        return copy

    echo_copies = [
        fetch(echo_hbm.at[:, :, pl.ds(part * h, part)], echo.at[h], 6 + h) for h in range(PARTS)
    ]
    chirp_copy = fetch(chirp_hbm, chirp, 1)
    shifts_copy = fetch(shifts_hbm, shifts, 2)
    index_copy = fetch(tap_index_hbm, tap_index, 3)
    table_copy = fetch(table_hbm, table, 4)
    trig_copy = fetch(trig_hbm.at[me], trig, 5)
    filt_copy = fetch(filt_hbm, filt, 0)

    barrier = pltpu.get_barrier_semaphore()

    def greet(k, carry):
        pl.semaphore_signal(
            barrier, inc=1, device_id=(lax.rem(me + k, n), g), device_id_type=MESH
        )
        return carry

    lax.fori_loop(1, n, greet, 0)
    for d in (1, 2, ng - 2, ng - 1):
        pl.semaphore_signal(barrier, inc=1, device_id=(me, lax.rem(g + d, ng)), device_id_type=MESH)

    def halo_copy(src, dst, slot, d):
        return pltpu.make_async_remote_copy(
            src_ref=src,
            dst_ref=dst,
            send_sem=halo_send.at[slot],
            recv_sem=halo_recv.at[slot],
            device_id=(me, lax.rem(g - d + ng, ng)),
            device_id_type=MESH,
        )

    odd = lax.rem(g, 2) == 1

    even = lax.rem(g, 2) == 0

    def later(h):
        return h >= 2

    def sends_echo(d, h):
        far_enough = g >= d
        return far_enough & odd if d == 2 and h < PASSED else far_enough

    def pass_on(h):
        return pltpu.make_async_remote_copy(
            src_ref=wide.at[:, pl.ds(cells + part * h, part)],
            dst_ref=wide.at[:, pl.ds(2 * cells + part * h, part)],
            send_sem=pass_send.at[h],
            recv_sem=halo_recv.at[PARTS + h],
            device_id=(me, lax.rem(g - 1 + ng, ng)),
            device_id_type=MESH,
        )

    passes_on = odd & (g + 1 < ng)

    def echo_copy_of(d, h):
        return halo_copy(
            wide.at[:, pl.ds(part * h, part)],
            wide.at[:, pl.ds(d * cells + part * h, part)],
            PARTS * (d - 1) + h,
            d,
        )

    for h in range(PARTS):
        echo_copies[h].wait()
        for s in range(groups):
            at = slice(HALF * s, HALF * (s + 1))
            wide[SUB * s : SUB * (s + 1), part * h : part * (h + 1)] = jnp.concatenate(
                [echo[h, 0, at, :], echo[h, 1, at, :]], axis=0
            ).astype(BF16)
        if h == 0:
            pl.semaphore_wait(barrier, n - 1 + 4)
        pl.when(sends_echo(1, h))(echo_copy_of(1, h).start)
        if not later(h):
            pl.when(sends_echo(2, h))(echo_copy_of(2, h).start)
        else:
            pl.when(sends_echo(2, h) & even)(echo_copy_of(2, h).start)

    chirp_copy.wait()
    span = chirp_len + 2 * block
    row_id = lax.broadcasted_iota(jnp.int32, (LANE, LANE), 0)
    col_id = lax.broadcasted_iota(jnp.int32, (LANE, LANE), 1)
    mirror = (row_id + col_id == LANE - 1).astype(BF16)
    pieces = [
        jnp.dot(chirp[:, LANE * i : LANE * (i + 1)], mirror, preferred_element_type=F32)
        for i in reversed(range(chirp_len // LANE))
    ]
    edge = jnp.zeros((2, block), F32)
    base = jnp.concatenate([edge] + pieces + [edge], axis=1)
    for c in range(2):
        copies = jnp.broadcast_to(base[c : c + 1], (LANE, span))
        band[c] = pltpu.roll(copies, 1, 1, stride=1, stride_axis=0).astype(BF16)
    for a in range((chirp_len + block) // LANE):
        start = chirp_len + block - LANE * a
        for c in range(2):
            weights[LANE * a : LANE * (a + 1), block * c : block * (c + 1)] = band[
                c, :, start : start + block
            ]

    shifts_copy.wait()
    index_copy.wait()
    table_copy.wait()
    phases = table.shape[1]
    on_row = lax.broadcasted_iota(jnp.int32, (2 * rows, rows), 0)
    on_col = lax.broadcasted_iota(jnp.int32, (2 * rows, rows), 1)
    row_of = lax.div(on_row, SUB) * HALF + lax.rem(on_row, HALF)

    def across(values):
        return jnp.broadcast_to(values.astype(F32).reshape(1, rows), (2 * rows, rows))

    def pick(mask, values):
        return jnp.sum(jnp.where(mask, values, 0.0), axis=1, keepdims=True)

    shift_row = across(shifts[...])
    shift = pick(row_of == on_col, shift_row)
    distant = shift >= float(cells)
    rank = pick(on_col < row_of, jnp.where(shift_row >= float(cells), 1.0, 0.0))
    plain_row = lax.broadcasted_iota(jnp.int32, (rows, rows), 0)
    plain_col = lax.broadcasted_iota(jnp.int32, (rows, rows), 1)

    def upright(values):
        spread_out = jnp.broadcast_to(values.astype(F32).reshape(1, rows), (rows, rows))
        return pick(plain_row == plain_col, spread_out)

    shift_wide[...] = jnp.broadcast_to(upright(shifts[...]).astype(jnp.int32), (rows, LANE))
    phase_id = lax.broadcasted_iota(jnp.int32, (rows, phases), 1).astype(F32)
    coefs = lax.dot_general(
        jnp.where(upright(tap_index[...]) == phase_id, 1.0, 0.0),
        table[...],
        (((1,), (1,)), ((), ())),
        precision=lax.Precision.HIGHEST,
        preferred_element_type=F32,
    )
    for q in range(coef_wide.shape[0]):
        coef_wide[q] = jnp.broadcast_to(coefs[:, q : q + 1], (rows, LANE))
    from_row = lax.broadcasted_iota(jnp.int32, (2 * rows, 2 * slots), 0)
    to_slot = lax.broadcasted_iota(jnp.int32, (2 * rows, 2 * slots), 1)
    same_part = lax.rem(lax.div(from_row, HALF), 2) == lax.rem(lax.div(to_slot, HALF), 2)
    slot_of = (lax.div(to_slot, SUB) * HALF + lax.rem(to_slot, HALF)).astype(F32)
    matches = jnp.where(rank == slot_of, 1.0, 0.0) * jnp.where(same_part, 1.0, 0.0)
    matches = matches * jnp.where(distant, 1.0, 0.0)
    spread[...] = matches.astype(BF16)
    gathering[...] = matches.T.astype(BF16)

    ny = n // nz
    my_y, my_z = lax.div(me, nz), lax.rem(me, nz)
    parity = lax.rem(me, 2)

    def away(i, count):
        return count // 2 + (1 - 2 * (i % 2)) * ((i + 1) // 2)

    all_zs = [lax.rem(my_z + away(i, nz), nz) for i in range(nz)]

    def place(y, z):
        spot = lax.div(z, 2)
        row = SUB * (nz // 2 // lanes) * y + SUB * lax.div(spot, lanes)
        return pl.multiple_of(row, SUB), pl.multiple_of(LANE * lax.rem(spot, lanes), LANE)

    def tile(ref, p):
        row, col = place(my_y, my_z)
        return ref.at[p, pl.ds(row, SUB), pl.ds(col, LANE)]

    def other(p):
        return lax.rem(parity + p, 2)

    def scatter(src, dst, phase, p):
        job = p // JOBS

        def send(y, z):
            row, col = place(y, z)
            pltpu.make_async_remote_copy(
                src_ref=src.at[p, pl.ds(row, SUB), pl.ds(col, LANE)],
                dst_ref=dst.at[job, me],
                send_sem=part_send.at[phase, p],
                recv_sem=job_recv.at[phase, job],
                device_id=(y * nz + z, g),
                device_id_type=MESH,
            ).start()

        zs = [lax.rem(my_z + 2 * away(i, nz // 2) + other(p), nz) for i in range(nz // 2)]

        def start(k, carry):
            y = lax.rem(my_y + away(k, ny), ny)
            for z in zs:
                send(y, z)
            return carry

        lax.fori_loop(0, ny - 1, start, 0)
        for z in zs[:-1]:
            send(my_y, z)
        pl.when(other(p) == 1)(lambda: send(my_y, zs[-1]))

        @pl.when(other(p) == 0)
        def _():
            pltpu.make_async_copy(
                tile(src, p), dst.at[job, me], job_recv.at[phase, job]
            ).start()

    def gather(src, dst, phase, job):
        p = 2 * job + parity

        target = tile(dst, p)

        def send(y, z):
            q = y * nz + z
            pltpu.make_async_remote_copy(
                src_ref=src.at[job, q],
                dst_ref=target,
                send_sem=job_send.at[phase, job],
                recv_sem=part_recv.at[phase, p],
                device_id=(q, g),
                device_id_type=MESH,
            ).start()

        def start(k, carry):
            y = lax.rem(my_y + away(k, ny), ny)
            for z in all_zs:
                send(y, z)
            return carry

        lax.fori_loop(0, ny - 1, start, 0)
        for z in all_zs[:-1]:
            send(my_y, z)
        pltpu.make_async_copy(src.at[job, me], target, part_recv.at[phase, p]).start()

    def scattered(dst, phase, job):
        pltpu.make_async_copy(dst.at[job], dst.at[job], job_recv.at[phase, job]).wait()

    def gathered(dst, phase, p):
        pltpu.make_async_copy(dst.at[p], dst.at[p], part_recv.at[phase, p]).wait()

    def transform(fft, src, dst, h):
        xs = []
        for p in range(n):
            value = decode(src[h, p])
            xs.append((value[:HALF], value[HALF:]))
        for p, (re, im) in enumerate(fft(xs)):
            dst[h, p] = encode(jnp.concatenate([re, im], axis=0) * (1.0 / math.sqrt(n)))

    def compress_near(h):
        reach = 2 * cells - part * h
        partial[h] = jnp.dot(
            wide[:, part * h : 2 * cells], weights[:reach, :], preferred_element_type=F32
        )

    def compress(h):
        reach = 2 * cells - part * h
        product = partial[h] + jnp.dot(
            wide[:, 2 * cells : part * h + chirp_len + block],
            weights[reach:, :],
            preferred_element_type=F32,
        )
        piece = product.reshape(groups, 2, HALF, 2 * block)
        real = piece[:, 0, :, :block] - piece[:, 1, :, block:]
        imag = piece[:, 0, :, block:] + piece[:, 1, :, :block]
        send_1[h] = encode(jnp.concatenate([real, imag], axis=1).reshape(2 * rows, block))

    def echo_arrived(d, h):
        pl.when(g + d < ng)(echo_copy_of(d, h).wait_recv)

        @pl.when(g + d >= ng)
        def _():
            start = d * cells + part * h
            wide[:, start : start + part] = jnp.zeros((2 * rows, part), BF16)

    for h in range(PARTS):
        echo_arrived(1, h)
        if h < PASSED:
            pl.when(passes_on)(pass_on(h).start)
        if h == 0:
            for i in range(PARTS):
                if later(i):
                    pl.when(sends_echo(2, i) & odd)(echo_copy_of(2, i).start)
    for h in range(PARTS):
        compress_near(h)
        echo_arrived(2, h)
        compress(h)
        scatter(send_1, recv_1, 0, h)

    for job in range(JOBS):
        scattered(recv_1, 0, job)
        transform(fft_forward, recv_1, send_2, job)
        gather(send_2, recv_2, 0, job)

    def times(at, upper, lower):
        return jnp.dot(
            jnp.concatenate([trig[at], trig[at + 1], trig[at]], axis=1),
            jnp.concatenate([upper, upper, lower], axis=0),
            preferred_element_type=F32,
        )

    def split(value):
        upper = value.astype(BF16)
        return upper, (value - upper.astype(F32)).astype(BF16)

    def spec_copy_of(d, h):
        src, dst = ((spec_code, halo_1), (far_code, halo_2))[d - 1]
        return halo_copy(src.at[h], dst.at[h], 2 * PARTS + PARTS * (d - 1) + h, d)

    trig_copy.wait()
    for h in range(PARTS):
        gathered(recv_2, 0, h)
        spectrum = times(0, *split(decode(recv_2[h])))
        code = encode(spectrum)
        spec_code[h] = code
        pl.when(g >= 1)(spec_copy_of(1, h).start)
        far_code[h] = jnp.dot(gathering[...], code, preferred_element_type=F32).astype(BF16)
        pl.when(g >= 2)(spec_copy_of(2, h).start)
        spec[:, part * h : part * (h + 1)] = spectrum

    def spec_arrived(d, h):
        dst = (halo_1, halo_2)[d - 1]
        pl.when(g + d < ng)(spec_copy_of(d, h).wait_recv)

        @pl.when(g + d >= ng)
        def _():
            dst[h] = jnp.zeros(dst.shape[1:], BF16)

        start = d * cells + part * h
        if d == 1:
            value = halo_1[h]
        else:
            value = jnp.dot(spread[...], halo_2[h], preferred_element_type=F32)
        spec[:, start : start + part] = decode(value)


    lane = lax.broadcasted_iota(jnp.int32, (HALF, LANE), 1)
    block_tiles = cells // LANE
    reach = cells // 2
    lanes_out = reach // LANE

    def ahead(xs, by):
        moved = [pltpu.roll(x, LANE - by, 1) for x in xs]
        kept = lane < LANE - by
        return [jnp.where(kept, a, b) for a, b in zip(moved, moved[1:])] + [moved[-1]]

    def migrate(h):
        start = reach * h

        def row_group(j):
            at = pl.multiple_of(SUB * j, SUB)
            own = pl.multiple_of(HALF * j, HALF)
            shift = shift_wide[pl.ds(own, HALF), :]
            distant = shift >= cells
            rest = jnp.where(distant, shift - cells, shift)
            fine = rest & (LANE - 1)
            turned = lane + fine
            inside = turned < LANE
            turned = jnp.where(inside, turned, turned - LANE)
            totals = []
            for c in range(2):
                row = pl.ds(pl.multiple_of(at + HALF * c, HALF), HALF)

                def load(t):
                    return spec[row, start + LANE * t : start + LANE * (t + 1)]

                count = lanes_out + block_tiles
                cur = [
                    jnp.where(distant, load(t + block_tiles), load(t)) for t in range(count)
                ]
                step = block_tiles // 2
                while step >= 1:
                    bit = (rest & (step * LANE)) != 0
                    width = lanes_out + step + 1
                    cur = [
                        jnp.where(bit, cur[min(t + step, count - 1)], cur[t]) for t in range(width)
                    ]
                    count = width
                    step //= 2
                cur = [jnp.take_along_axis(x, turned, axis=1) for x in cur]
                cur = [jnp.where(inside, cur[t], cur[t + 1]) for t in range(lanes_out + 1)]
                weight = [coef_wide[q, pl.ds(own, HALF), :] for q in range(8)]
                four = ahead(cur, 4)
                pair = [
                    [weight[q] * x + weight[q + 4] * y for x, y in zip(cur, four)]
                    for q in range(4)
                ]
                even = [x + y for x, y in zip(pair[0], ahead(pair[2], 2))]
                odd = [x + y for x, y in zip(pair[1], ahead(pair[3], 2))]
                total = [x + y for x, y in zip(even, ahead(odd, 1))]
                totals.append(total)
            for t in range(lanes_out):
                col = slice(start + LANE * t, start + LANE * (t + 1))
                fr = filt[0, pl.ds(own, HALF), col]
                fi = filt[1, pl.ds(own, HALF), col]
                x, y = totals[0][t], totals[1][t]
                both = jnp.concatenate([x * fr - y * fi, x * fi + y * fr], axis=0)
                upper, lower = split(both)
                high[pl.ds(at, SUB), col] = upper
                low[pl.ds(at, SUB), col] = lower

        def some(j, carry):
            for u in range(UNROLL):
                row_group(UNROLL * j + u)
            return carry

        lax.fori_loop(0, groups // UNROLL, some, 0)

    for h in range(PARTS):
        spec_arrived(1, h)
    filt_copy.wait()
    for h in range(PARTS):
        if h % 2 == 0:
            spec_arrived(2, h)
            spec_arrived(2, h + 1)
            migrate(h // 2)
        col = slice(part * h, part * (h + 1))
        send_3[h] = encode(times(2, high[:, col], low[:, col]))
        scatter(send_3, recv_3, 1, h)

    for job in range(JOBS):
        scattered(recv_3, 1, job)
        transform(fft_inverse, recv_3, send_4, job)
        gather(send_4, recv_4, 1, job)
    for h in range(PARTS):
        gathered(recv_4, 1, h)
        for s in range(groups):
            value = decode(recv_4[h, SUB * s : SUB * (s + 1), :])
            for c in range(2):
                out[c, HALF * s : HALF * (s + 1), part * h : part * (h + 1)] = value[
                    HALF * c : HALF * (c + 1)
                ]

    for h in range(PASSED):
        pl.when(passes_on)(pass_on(h).wait_send)
    for d in (1, 2):
        for h in range(PARTS):
            pl.when(sends_echo(d, h))(echo_copy_of(d, h).wait_send)
            pl.when(g >= d)(spec_copy_of(d, h).wait_send)
    for phase in range(2):
        for job in range(JOBS):
            sent = send_2.at[0, pl.ds(0, n - 1)]
            pltpu.make_async_copy(sent, sent, job_send.at[phase, job]).wait()
        for p in range(PARTS):
            for same in (0, 1):
                sent = send_2.at[0, pl.ds(0, n // 2 - 1 + same)]
                pl.when(other(p) == same)(
                    pltpu.make_async_copy(sent, sent, part_send.at[phase, p]).wait
                )


def solution(mesh):
    n, ng = mesh.shape["az"], mesh.shape["rg"]

    def local(echo_field, range_chirp, azimuth_filter, shifts, tap_index, taps_table):
        rows, cells = echo_field.shape[1], echo_field.shape[2]
        chirp_len = range_chirp.shape[1]
        phases, taps = taps_table.shape
        block = 256
        slots = rows // 2
        part = cells // PARTS
        trig = jnp.asarray(trig_tables(n, rows))
        stack = (2, rows, cells)
        flat = (PARTS, 2 * rows, part)
        tiles = (JOBS, n, SUB, LANE)
        hbm = pl.BlockSpec(memory_space=pltpu.HBM)
        return pl.pallas_call(
            functools.partial(kernel, n, ng, slots),
            out_shape=pltpu.VMEM(stack, F32),
            in_specs=[hbm] * 7,
            out_specs=pl.BlockSpec(memory_space=pltpu.VMEM),
            scratch_shapes=[
                pltpu.VMEM((PARTS, 2, rows, part), F32),
                pltpu.VMEM((2, chirp_len), BF16),
                pltpu.VMEM(stack, F32),
                pltpu.VMEM((rows,), jnp.int32),
                pltpu.VMEM((rows,), jnp.int32),
                pltpu.VMEM((taps, phases), F32),
                pltpu.VMEM((4, 2 * rows, 2 * rows), BF16),
                pltpu.VMEM((2, LANE, chirp_len + 2 * block), BF16),
                pltpu.VMEM((chirp_len + block, 2 * block), BF16),
                pltpu.VMEM((2 * rows, 3 * cells), BF16),
                pltpu.VMEM((PARTS, 2 * rows, 2 * block), F32),
                pltpu.VMEM((rows, LANE), jnp.int32),
                pltpu.VMEM((taps, rows, LANE), F32),
                pltpu.VMEM((2 * rows, 2 * slots), BF16),
                pltpu.VMEM((2 * slots, 2 * rows), BF16),
                pltpu.VMEM(flat, BF16),
                pltpu.VMEM(tiles, BF16),
                pltpu.VMEM(tiles, BF16),
                pltpu.VMEM(flat, BF16),
                pltpu.VMEM((2 * rows, 3 * cells), F32),
                pltpu.VMEM(flat, BF16),
                pltpu.VMEM((PARTS, 2 * slots, part), BF16),
                pltpu.VMEM(flat, BF16),
                pltpu.VMEM((PARTS, 2 * slots, part), BF16),
                pltpu.VMEM((2 * rows, cells), BF16),
                pltpu.VMEM((2 * rows, cells), BF16),
                pltpu.VMEM(flat, BF16),
                pltpu.VMEM(tiles, BF16),
                pltpu.VMEM(tiles, BF16),
                pltpu.VMEM(flat, BF16),
                pltpu.SemaphoreType.DMA((6 + PARTS,)),
                pltpu.SemaphoreType.DMA((4 * PARTS,)),
                pltpu.SemaphoreType.DMA((4 * PARTS,)),
                pltpu.SemaphoreType.DMA((PASSED,)),
                pltpu.SemaphoreType.DMA((2, PARTS)),
                pltpu.SemaphoreType.DMA((2, PARTS)),
                pltpu.SemaphoreType.DMA((2, JOBS)),
                pltpu.SemaphoreType.DMA((2, JOBS)),
            ],
            compiler_params=pltpu.CompilerParams(
                collective_id=0, has_side_effects=True, vmem_limit_bytes=48 * 1024 * 1024
            ),
            cost_estimate=pl.CostEstimate(
                flops=1_600_000_000, bytes_accessed=2_000_000, transcendentals=0
            ),
        )(
            *(
                pltpu.with_memory_space_constraint(x, pltpu.HBM)
                for x in (
                    echo_field,
                    range_chirp,
                    azimuth_filter,
                    shifts,
                    tap_index,
                    taps_table.T,
                    trig,
                )
            )
        )

    placed = (P(None, "az", "rg"), P(), P(None, "az", "rg"), P("az"), P("az"), P())
    return jax.shard_map(
        local, mesh=mesh, in_specs=placed, out_specs=P(None, "az", "rg"), check_vma=False
    )
```

```python
import functools
import math

import jax
import jax.numpy as jnp
import numpy as np
from jax import lax
from jax.experimental import pallas as pl
from jax.experimental.pallas import tpu as pltpu
from jax.sharding import PartitionSpec as P

MESH = pl.DeviceIdType.MESH
F32 = jnp.float32
BF16 = jnp.bfloat16
LANE = 128
SUB = 16
HALF = 8
PARTS = 4
JOBS = 2
PASSED = 3
UNROLL = 4


def encode(x):
    return (x * jnp.abs(x)).astype(BF16)


def decode(code):
    c = code.astype(F32)
    return c * lax.rsqrt(jnp.maximum(jnp.abs(c), 1e-37))


def bit_reverse(value, bits):
    result = 0
    for position in range(bits):
        result += ((value >> position) & 1) << (bits - 1 - position)
    return result


def turn(pair, k, n, sign):
    re, im = pair
    if k == 0:
        return re, im
    if 4 * k == n:
        return (-im, re) if sign > 0 else (im, -re)
    c = math.cos(2 * math.pi * k / n)
    s = sign * math.sin(2 * math.pi * k / n)
    if 8 * k == n:
        return ((re - im) * c, (re + im) * c) if sign > 0 else ((re + im) * c, (im - re) * c)
    if 8 * k == 3 * n:
        h = -c
        return (-(re + im) * h, (re - im) * h) if sign > 0 else ((im - re) * h, -(re + im) * h)
    return re * c - im * s, re * s + im * c


def fft_forward(xs):
    n = len(xs)
    if n == 1:
        return xs
    half = n // 2
    low, high = [], []
    for k in range(half):
        (ar, ai), (br, bi) = xs[k], xs[k + half]
        low.append((ar + br, ai + bi))
        high.append(turn((ar - br, ai - bi), k, n, -1))
    return fft_forward(low) + fft_forward(high)


def fft_inverse(xs):
    n = len(xs)
    if n == 1:
        return xs
    half = n // 2
    low = fft_inverse(xs[:half])
    high = fft_inverse(xs[half:])
    first, second = [], []
    for k in range(half):
        ar, ai = low[k]
        br, bi = turn(high[k], k, n, 1)
        first.append((ar + br, ai + bi))
        second.append((ar - br, ai - bi))
    return first + second


def packed(rows):
    group, part, inner = np.meshgrid(
        np.arange(rows // HALF), np.arange(2), np.arange(HALF), indexing="ij"
    )
    return (part * rows + group * HALF + inner).reshape(-1)


def trig_tables(n_az, rows):
    total = n_az * rows
    bits = n_az.bit_length() - 1
    order = packed(rows)
    tables = np.zeros((n_az, 4, 2 * rows, 2 * rows), np.float32)
    s = np.arange(rows)[None, :]
    j = np.arange(rows)[:, None]
    for p in range(n_az):
        b = bit_reverse(p, bits)
        angle = 2 * np.pi * ((s * (b + n_az * j)) % total) / total
        c, d = np.cos(angle) / math.sqrt(rows), np.sin(angle) / math.sqrt(rows)
        m = np.block([[c, d], [-d, c]])[np.ix_(order, order)]
        for at, mat in ((0, m), (2, m.T)):
            high = mat.astype(np.float32).astype(jnp.bfloat16)
            tables[p, at] = high.astype(np.float32)
            tables[p, at + 1] = mat - high.astype(np.float64)
    return tables.astype(jnp.bfloat16)


def kernel(
    n,
    ng,
    slots,
    echo_hbm,
    chirp_hbm,
    filt_hbm,
    shifts_hbm,
    tap_index_hbm,
    table_hbm,
    trig_hbm,
    out,
    echo,
    chirp,
    filt,
    shifts,
    tap_index,
    table,
    trig,
    band,
    weights,
    wide,
    partial,
    shift_wide,
    coef_wide,
    spread,
    gathering,
    send_1,
    recv_1,
    send_2,
    recv_2,
    spec,
    spec_code,
    far_code,
    halo_1,
    halo_2,
    high,
    low,
    send_3,
    recv_3,
    send_4,
    recv_4,
    local_sem,
    halo_send,
    halo_recv,
    pass_send,
    part_send,
    part_recv,
    job_send,
    job_recv,
    round_1,
    round_2,
):
    rows, cells = filt.shape[1], filt.shape[2]
    chirp_len = chirp.shape[1]
    part = cells // PARTS
    lanes = part // LANE
    groups = rows // HALF
    block = 256
    nz = 8
    me = lax.axis_index("az")
    g = lax.axis_index("rg")

    def fetch(src, dst, at):
        copy = pltpu.make_async_copy(src, dst, local_sem.at[at])
        copy.start()
        return copy

    echo_copies = [
        fetch(echo_hbm.at[:, :, pl.ds(part * h, part)], echo.at[h], 6 + h) for h in range(PARTS)
    ]

    ny = n // nz
    my_y, my_z = lax.div(me, nz), lax.rem(me, nz)
    def away(i, count):
        return count // 2 + (1 - 2 * (i % 2)) * ((i + 1) // 2)

    all_zs = [lax.rem(my_z + away(i, nz), nz) for i in range(nz)]
    barrier = pltpu.get_barrier_semaphore()

    near = [(lax.rem(my_y + d, ny), my_z) for d in range(1, ny)]
    near = near + [(my_y, lax.rem(my_z + d, nz)) for d in (1, 2, nz - 2, nz - 1)]

    def tell(semaphore):
        for y, z in near:
            pl.semaphore_signal(semaphore, inc=1, device_id=(y * nz + z, g), device_id_type=MESH)

    for d in (1, 2, ng - 2, ng - 1):
        pl.semaphore_signal(barrier, inc=1, device_id=(me, lax.rem(g + d, ng)), device_id_type=MESH)
    tell(barrier)

    chirp_copy = fetch(chirp_hbm, chirp, 1)
    shifts_copy = fetch(shifts_hbm, shifts, 2)
    index_copy = fetch(tap_index_hbm, tap_index, 3)
    table_copy = fetch(table_hbm, table, 4)
    trig_copy = fetch(trig_hbm.at[me], trig, 5)
    filt_copy = fetch(filt_hbm, filt, 0)

    def halo_copy(src, dst, slot, d):
        return pltpu.make_async_remote_copy(
            src_ref=src,
            dst_ref=dst,
            send_sem=halo_send.at[slot],
            recv_sem=halo_recv.at[slot],
            device_id=(me, lax.rem(g - d + ng, ng)),
            device_id_type=MESH,
        )

    odd = lax.rem(g, 2) == 1

    even = lax.rem(g, 2) == 0

    def later(h):
        return h >= 2

    def sends_echo(d, h):
        far_enough = g >= d
        return far_enough & odd if d == 2 and h < PASSED else far_enough

    def pass_on(h):
        return pltpu.make_async_remote_copy(
            src_ref=wide.at[:, pl.ds(cells + part * h, part)],
            dst_ref=wide.at[:, pl.ds(2 * cells + part * h, part)],
            send_sem=pass_send.at[h],
            recv_sem=halo_recv.at[PARTS + h],
            device_id=(me, lax.rem(g - 1 + ng, ng)),
            device_id_type=MESH,
        )

    passes_on = odd & (g + 1 < ng)

    def echo_copy_of(d, h):
        return halo_copy(
            wide.at[:, pl.ds(part * h, part)],
            wide.at[:, pl.ds(d * cells + part * h, part)],
            PARTS * (d - 1) + h,
            d,
        )

    for h in range(PARTS):
        echo_copies[h].wait()
        for s in range(groups):
            at = slice(HALF * s, HALF * (s + 1))
            wide[SUB * s : SUB * (s + 1), part * h : part * (h + 1)] = jnp.concatenate(
                [echo[h, 0, at, :], echo[h, 1, at, :]], axis=0
            ).astype(BF16)
        if h == 0:
            pl.semaphore_wait(barrier, 4 + len(near))
            tell(round_1)
        pl.when(sends_echo(1, h))(echo_copy_of(1, h).start)
        if not later(h):
            pl.when(sends_echo(2, h))(echo_copy_of(2, h).start)
        else:
            pl.when(sends_echo(2, h) & even)(echo_copy_of(2, h).start)

    chirp_copy.wait()
    span = chirp_len + 2 * block
    row_id = lax.broadcasted_iota(jnp.int32, (LANE, LANE), 0)
    col_id = lax.broadcasted_iota(jnp.int32, (LANE, LANE), 1)
    mirror = (row_id + col_id == LANE - 1).astype(BF16)
    pieces = [
        jnp.dot(chirp[:, LANE * i : LANE * (i + 1)], mirror, preferred_element_type=F32)
        for i in reversed(range(chirp_len // LANE))
    ]
    edge = jnp.zeros((2, block), F32)
    base = jnp.concatenate([edge] + pieces + [edge], axis=1)
    for c in range(2):
        copies = jnp.broadcast_to(base[c : c + 1], (LANE, span))
        band[c] = pltpu.roll(copies, 1, 1, stride=1, stride_axis=0).astype(BF16)
    for a in range((chirp_len + block) // LANE):
        start = chirp_len + block - LANE * a
        for c in range(2):
            weights[LANE * a : LANE * (a + 1), block * c : block * (c + 1)] = band[
                c, :, start : start + block
            ]

    pl.semaphore_wait(round_1, len(near))
    tell(round_2)

    shifts_copy.wait()
    index_copy.wait()
    table_copy.wait()
    phases = table.shape[1]
    on_row = lax.broadcasted_iota(jnp.int32, (2 * rows, rows), 0)
    on_col = lax.broadcasted_iota(jnp.int32, (2 * rows, rows), 1)
    row_of = lax.div(on_row, SUB) * HALF + lax.rem(on_row, HALF)

    def across(values):
        return jnp.broadcast_to(values.astype(F32).reshape(1, rows), (2 * rows, rows))

    def pick(mask, values):
        return jnp.sum(jnp.where(mask, values, 0.0), axis=1, keepdims=True)

    shift_row = across(shifts[...])
    shift = pick(row_of == on_col, shift_row)
    distant = shift >= float(cells)
    rank = pick(on_col < row_of, jnp.where(shift_row >= float(cells), 1.0, 0.0))
    plain_row = lax.broadcasted_iota(jnp.int32, (rows, rows), 0)
    plain_col = lax.broadcasted_iota(jnp.int32, (rows, rows), 1)

    def upright(values):
        spread_out = jnp.broadcast_to(values.astype(F32).reshape(1, rows), (rows, rows))
        return pick(plain_row == plain_col, spread_out)

    shift_wide[...] = jnp.broadcast_to(upright(shifts[...]).astype(jnp.int32), (rows, LANE))
    phase_id = lax.broadcasted_iota(jnp.int32, (rows, phases), 1).astype(F32)
    coefs = lax.dot_general(
        jnp.where(upright(tap_index[...]) == phase_id, 1.0, 0.0),
        table[...],
        (((1,), (1,)), ((), ())),
        precision=lax.Precision.HIGHEST,
        preferred_element_type=F32,
    )
    for q in range(coef_wide.shape[0]):
        coef_wide[q] = jnp.broadcast_to(coefs[:, q : q + 1], (rows, LANE))
    from_row = lax.broadcasted_iota(jnp.int32, (2 * rows, 2 * slots), 0)
    to_slot = lax.broadcasted_iota(jnp.int32, (2 * rows, 2 * slots), 1)
    same_part = lax.rem(lax.div(from_row, HALF), 2) == lax.rem(lax.div(to_slot, HALF), 2)
    slot_of = (lax.div(to_slot, SUB) * HALF + lax.rem(to_slot, HALF)).astype(F32)
    matches = jnp.where(rank == slot_of, 1.0, 0.0) * jnp.where(same_part, 1.0, 0.0)
    matches = matches * jnp.where(distant, 1.0, 0.0)
    spread[...] = matches.astype(BF16)
    gathering[...] = matches.T.astype(BF16)

    parity = lax.rem(me, 2)

    def place(y, z):
        spot = lax.div(z, 2)
        row = SUB * (nz // 2 // lanes) * y + SUB * lax.div(spot, lanes)
        return pl.multiple_of(row, SUB), pl.multiple_of(LANE * lax.rem(spot, lanes), LANE)

    def tile(ref, p):
        row, col = place(my_y, my_z)
        return ref.at[p, pl.ds(row, SUB), pl.ds(col, LANE)]

    def other(p):
        return lax.rem(parity + p, 2)

    def scatter(src, dst, phase, p):
        job = p // JOBS

        def send(y, z):
            row, col = place(y, z)
            pltpu.make_async_remote_copy(
                src_ref=src.at[p, pl.ds(row, SUB), pl.ds(col, LANE)],
                dst_ref=dst.at[job, me],
                send_sem=part_send.at[phase, p],
                recv_sem=job_recv.at[phase, job],
                device_id=(y * nz + z, g),
                device_id_type=MESH,
            ).start()

        zs = [lax.rem(my_z + 2 * away(i, nz // 2) + other(p), nz) for i in range(nz // 2)]

        def start(k, carry):
            y = lax.rem(my_y + away(k, ny), ny)
            for z in zs:
                send(y, z)
            return carry

        lax.fori_loop(0, ny - 1, start, 0)
        for z in zs[:-1]:
            send(my_y, z)
        pl.when(other(p) == 1)(lambda: send(my_y, zs[-1]))

        @pl.when(other(p) == 0)
        def _():
            pltpu.make_async_copy(
                tile(src, p), dst.at[job, me], job_recv.at[phase, job]
            ).start()

    def gather(src, dst, phase, job):
        p = 2 * job + parity

        target = tile(dst, p)

        def send(y, z):
            q = y * nz + z
            pltpu.make_async_remote_copy(
                src_ref=src.at[job, q],
                dst_ref=target,
                send_sem=job_send.at[phase, job],
                recv_sem=part_recv.at[phase, p],
                device_id=(q, g),
                device_id_type=MESH,
            ).start()

        def start(k, carry):
            y = lax.rem(my_y + away(k, ny), ny)
            for z in all_zs:
                send(y, z)
            return carry

        lax.fori_loop(0, ny - 1, start, 0)
        for z in all_zs[:-1]:
            send(my_y, z)
        pltpu.make_async_copy(src.at[job, me], target, part_recv.at[phase, p]).start()

    def scattered(dst, phase, job):
        pltpu.make_async_copy(dst.at[job], dst.at[job], job_recv.at[phase, job]).wait()

    def gathered(dst, phase, p):
        pltpu.make_async_copy(dst.at[p], dst.at[p], part_recv.at[phase, p]).wait()

    def transform(fft, src, dst, h):
        xs = []
        for p in range(n):
            value = decode(src[h, p])
            xs.append((value[:HALF], value[HALF:]))
        for p, (re, im) in enumerate(fft(xs)):
            dst[h, p] = encode(jnp.concatenate([re, im], axis=0) * (1.0 / math.sqrt(n)))

    def compress_near(h):
        reach = 2 * cells - part * h
        partial[h] = jnp.dot(
            wide[:, part * h : 2 * cells], weights[:reach, :], preferred_element_type=F32
        )

    def compress(h):
        reach = 2 * cells - part * h
        product = partial[h] + jnp.dot(
            wide[:, 2 * cells : part * h + chirp_len + block],
            weights[reach:, :],
            preferred_element_type=F32,
        )
        piece = product.reshape(groups, 2, HALF, 2 * block)
        real = piece[:, 0, :, :block] - piece[:, 1, :, block:]
        imag = piece[:, 0, :, block:] + piece[:, 1, :, :block]
        send_1[h] = encode(jnp.concatenate([real, imag], axis=1).reshape(2 * rows, block))

    def echo_arrived(d, h):
        pl.when(g + d < ng)(echo_copy_of(d, h).wait_recv)

        @pl.when(g + d >= ng)
        def _():
            start = d * cells + part * h
            wide[:, start : start + part] = jnp.zeros((2 * rows, part), BF16)

    for h in range(PARTS):
        echo_arrived(1, h)
        if h < PASSED:
            pl.when(passes_on)(pass_on(h).start)
        if h == 0:
            for i in range(PARTS):
                if later(i):
                    pl.when(sends_echo(2, i) & odd)(echo_copy_of(2, i).start)
    pl.semaphore_wait(round_2, len(near))
    for h in range(PARTS):
        compress_near(h)
        echo_arrived(2, h)
        compress(h)
        scatter(send_1, recv_1, 0, h)

    for job in range(JOBS):
        scattered(recv_1, 0, job)
        transform(fft_forward, recv_1, send_2, job)
        gather(send_2, recv_2, 0, job)

    def times(at, upper, lower):
        return jnp.dot(
            jnp.concatenate([trig[at], trig[at + 1], trig[at]], axis=1),
            jnp.concatenate([upper, upper, lower], axis=0),
            preferred_element_type=F32,
        )

    def split(value):
        upper = value.astype(BF16)
        return upper, (value - upper.astype(F32)).astype(BF16)

    def spec_copy_of(d, h):
        src, dst = ((spec_code, halo_1), (far_code, halo_2))[d - 1]
        return halo_copy(src.at[h], dst.at[h], 2 * PARTS + PARTS * (d - 1) + h, d)

    trig_copy.wait()
    for h in range(PARTS):
        gathered(recv_2, 0, h)
        spectrum = times(0, *split(decode(recv_2[h])))
        code = encode(spectrum)
        spec_code[h] = code
        pl.when(g >= 1)(spec_copy_of(1, h).start)
        far_code[h] = jnp.dot(gathering[...], code, preferred_element_type=F32).astype(BF16)
        pl.when(g >= 2)(spec_copy_of(2, h).start)
        spec[:, part * h : part * (h + 1)] = spectrum

    def spec_arrived(d, h):
        dst = (halo_1, halo_2)[d - 1]
        pl.when(g + d < ng)(spec_copy_of(d, h).wait_recv)

        @pl.when(g + d >= ng)
        def _():
            dst[h] = jnp.zeros(dst.shape[1:], BF16)

        start = d * cells + part * h
        if d == 1:
            value = halo_1[h]
        else:
            value = jnp.dot(spread[...], halo_2[h], preferred_element_type=F32)
        spec[:, start : start + part] = decode(value)


    lane = lax.broadcasted_iota(jnp.int32, (HALF, LANE), 1)
    block_tiles = cells // LANE
    reach = cells // 2
    lanes_out = reach // LANE

    def ahead(xs, by):
        moved = [pltpu.roll(x, LANE - by, 1) for x in xs]
        kept = lane < LANE - by
        return [jnp.where(kept, a, b) for a, b in zip(moved, moved[1:])] + [moved[-1]]

    def migrate(h):
        start = reach * h

        def row_group(j):
            at = pl.multiple_of(SUB * j, SUB)
            own = pl.multiple_of(HALF * j, HALF)
            shift = shift_wide[pl.ds(own, HALF), :]
            distant = shift >= cells
            rest = jnp.where(distant, shift - cells, shift)
            fine = rest & (LANE - 1)
            turned = lane + fine
            inside = turned < LANE
            turned = jnp.where(inside, turned, turned - LANE)
            totals = []
            for c in range(2):
                row = pl.ds(pl.multiple_of(at + HALF * c, HALF), HALF)

                def load(t):
                    return spec[row, start + LANE * t : start + LANE * (t + 1)]

                count = lanes_out + block_tiles
                cur = [
                    jnp.where(distant, load(t + block_tiles), load(t)) for t in range(count)
                ]
                step = block_tiles // 2
                while step >= 1:
                    bit = (rest & (step * LANE)) != 0
                    width = lanes_out + step + 1
                    cur = [
                        jnp.where(bit, cur[min(t + step, count - 1)], cur[t]) for t in range(width)
                    ]
                    count = width
                    step //= 2
                cur = [jnp.take_along_axis(x, turned, axis=1) for x in cur]
                cur = [jnp.where(inside, cur[t], cur[t + 1]) for t in range(lanes_out + 1)]
                weight = [coef_wide[q, pl.ds(own, HALF), :] for q in range(8)]
                four = ahead(cur, 4)
                pair = [
                    [weight[q] * x + weight[q + 4] * y for x, y in zip(cur, four)]
                    for q in range(4)
                ]
                even = [x + y for x, y in zip(pair[0], ahead(pair[2], 2))]
                odd = [x + y for x, y in zip(pair[1], ahead(pair[3], 2))]
                total = [x + y for x, y in zip(even, ahead(odd, 1))]
                totals.append(total)
            for t in range(lanes_out):
                col = slice(start + LANE * t, start + LANE * (t + 1))
                fr = filt[0, pl.ds(own, HALF), col]
                fi = filt[1, pl.ds(own, HALF), col]
                x, y = totals[0][t], totals[1][t]
                both = jnp.concatenate([x * fr - y * fi, x * fi + y * fr], axis=0)
                upper, lower = split(both)
                high[pl.ds(at, SUB), col] = upper
                low[pl.ds(at, SUB), col] = lower

        def some(j, carry):
            for u in range(UNROLL):
                row_group(UNROLL * j + u)
            return carry

        lax.fori_loop(0, groups // UNROLL, some, 0)

    for h in range(PARTS):
        spec_arrived(1, h)
    filt_copy.wait()
    for h in range(PARTS):
        if h % 2 == 0:
            spec_arrived(2, h)
            spec_arrived(2, h + 1)
            migrate(h // 2)
        col = slice(part * h, part * (h + 1))
        send_3[h] = encode(times(2, high[:, col], low[:, col]))
        scatter(send_3, recv_3, 1, h)

    for job in range(JOBS):
        scattered(recv_3, 1, job)
        transform(fft_inverse, recv_3, send_4, job)
        gather(send_4, recv_4, 1, job)
    for h in range(PARTS):
        gathered(recv_4, 1, h)
        for s in range(groups):
            value = decode(recv_4[h, SUB * s : SUB * (s + 1), :])
            for c in range(2):
                out[c, HALF * s : HALF * (s + 1), part * h : part * (h + 1)] = value[
                    HALF * c : HALF * (c + 1)
                ]

    for h in range(PASSED):
        pl.when(passes_on)(pass_on(h).wait_send)
    for d in (1, 2):
        for h in range(PARTS):
            pl.when(sends_echo(d, h))(echo_copy_of(d, h).wait_send)
            pl.when(g >= d)(spec_copy_of(d, h).wait_send)
    for phase in range(2):
        for job in range(JOBS):
            sent = send_2.at[0, pl.ds(0, n - 1)]
            pltpu.make_async_copy(sent, sent, job_send.at[phase, job]).wait()
        for p in range(PARTS):
            for same in (0, 1):
                sent = send_2.at[0, pl.ds(0, n // 2 - 1 + same)]
                pl.when(other(p) == same)(
                    pltpu.make_async_copy(sent, sent, part_send.at[phase, p]).wait
                )


def solution(mesh):
    n, ng = mesh.shape["az"], mesh.shape["rg"]

    def local(echo_field, range_chirp, azimuth_filter, shifts, tap_index, taps_table):
        rows, cells = echo_field.shape[1], echo_field.shape[2]
        chirp_len = range_chirp.shape[1]
        phases, taps = taps_table.shape
        block = 256
        slots = rows // 2
        part = cells // PARTS
        trig = jnp.asarray(trig_tables(n, rows))
        stack = (2, rows, cells)
        flat = (PARTS, 2 * rows, part)
        tiles = (JOBS, n, SUB, LANE)
        hbm = pl.BlockSpec(memory_space=pltpu.HBM)
        return pl.pallas_call(
            functools.partial(kernel, n, ng, slots),
            out_shape=pltpu.VMEM(stack, F32),
            in_specs=[hbm] * 7,
            out_specs=pl.BlockSpec(memory_space=pltpu.VMEM),
            scratch_shapes=[
                pltpu.VMEM((PARTS, 2, rows, part), F32),
                pltpu.VMEM((2, chirp_len), BF16),
                pltpu.VMEM(stack, F32),
                pltpu.VMEM((rows,), jnp.int32),
                pltpu.VMEM((rows,), jnp.int32),
                pltpu.VMEM((taps, phases), F32),
                pltpu.VMEM((4, 2 * rows, 2 * rows), BF16),
                pltpu.VMEM((2, LANE, chirp_len + 2 * block), BF16),
                pltpu.VMEM((chirp_len + block, 2 * block), BF16),
                pltpu.VMEM((2 * rows, 3 * cells), BF16),
                pltpu.VMEM((PARTS, 2 * rows, 2 * block), F32),
                pltpu.VMEM((rows, LANE), jnp.int32),
                pltpu.VMEM((taps, rows, LANE), F32),
                pltpu.VMEM((2 * rows, 2 * slots), BF16),
                pltpu.VMEM((2 * slots, 2 * rows), BF16),
                pltpu.VMEM(flat, BF16),
                pltpu.VMEM(tiles, BF16),
                pltpu.VMEM(tiles, BF16),
                pltpu.VMEM(flat, BF16),
                pltpu.VMEM((2 * rows, 3 * cells), F32),
                pltpu.VMEM(flat, BF16),
                pltpu.VMEM((PARTS, 2 * slots, part), BF16),
                pltpu.VMEM(flat, BF16),
                pltpu.VMEM((PARTS, 2 * slots, part), BF16),
                pltpu.VMEM((2 * rows, cells), BF16),
                pltpu.VMEM((2 * rows, cells), BF16),
                pltpu.VMEM(flat, BF16),
                pltpu.VMEM(tiles, BF16),
                pltpu.VMEM(tiles, BF16),
                pltpu.VMEM(flat, BF16),
                pltpu.SemaphoreType.DMA((6 + PARTS,)),
                pltpu.SemaphoreType.DMA((4 * PARTS,)),
                pltpu.SemaphoreType.DMA((4 * PARTS,)),
                pltpu.SemaphoreType.DMA((PASSED,)),
                pltpu.SemaphoreType.DMA((2, PARTS)),
                pltpu.SemaphoreType.DMA((2, PARTS)),
                pltpu.SemaphoreType.DMA((2, JOBS)),
                pltpu.SemaphoreType.DMA((2, JOBS)),
                pltpu.SemaphoreType.REGULAR,
                pltpu.SemaphoreType.REGULAR,
            ],
            compiler_params=pltpu.CompilerParams(
                collective_id=0, has_side_effects=True, vmem_limit_bytes=48 * 1024 * 1024
            ),
            cost_estimate=pl.CostEstimate(
                flops=1_600_000_000, bytes_accessed=2_000_000, transcendentals=0
            ),
        )(
            *(
                pltpu.with_memory_space_constraint(x, pltpu.HBM)
                for x in (
                    echo_field,
                    range_chirp,
                    azimuth_filter,
                    shifts,
                    tap_index,
                    taps_table.T,
                    trig,
                )
            )
        )

    placed = (P(None, "az", "rg"), P(), P(None, "az", "rg"), P("az"), P("az"), P())
    return jax.shard_map(
        local, mesh=mesh, in_specs=placed, out_specs=P(None, "az", "rg"), check_vma=False
    )
```

```python
import functools
import math

import jax
import jax.numpy as jnp
import numpy as np
from jax import lax
from jax.experimental import pallas as pl
from jax.experimental.pallas import tpu as pltpu
from jax.sharding import PartitionSpec as P

MESH = pl.DeviceIdType.MESH
F32 = jnp.float32
BF16 = jnp.bfloat16
LANE = 128
SUB = 16
HALF = 8
PARTS = 4
JOBS = 2
PASSED = 3
UNROLL = 4


def encode(x):
    return (x * jnp.abs(x)).astype(BF16)


def decode(code):
    c = code.astype(F32)
    return c * lax.rsqrt(jnp.maximum(jnp.abs(c), 1e-37))


def bit_reverse(value, bits):
    result = 0
    for position in range(bits):
        result += ((value >> position) & 1) << (bits - 1 - position)
    return result


def turn(pair, k, n, sign):
    re, im = pair
    if k == 0:
        return re, im
    if 4 * k == n:
        return (-im, re) if sign > 0 else (im, -re)
    c = math.cos(2 * math.pi * k / n)
    s = sign * math.sin(2 * math.pi * k / n)
    if 8 * k == n:
        return ((re - im) * c, (re + im) * c) if sign > 0 else ((re + im) * c, (im - re) * c)
    if 8 * k == 3 * n:
        h = -c
        return (-(re + im) * h, (re - im) * h) if sign > 0 else ((im - re) * h, -(re + im) * h)
    return re * c - im * s, re * s + im * c


def fft_forward(xs):
    n = len(xs)
    if n == 1:
        return xs
    half = n // 2
    low, high = [], []
    for k in range(half):
        (ar, ai), (br, bi) = xs[k], xs[k + half]
        low.append((ar + br, ai + bi))
        high.append(turn((ar - br, ai - bi), k, n, -1))
    return fft_forward(low) + fft_forward(high)


def fft_inverse(xs):
    n = len(xs)
    if n == 1:
        return xs
    half = n // 2
    low = fft_inverse(xs[:half])
    high = fft_inverse(xs[half:])
    first, second = [], []
    for k in range(half):
        ar, ai = low[k]
        br, bi = turn(high[k], k, n, 1)
        first.append((ar + br, ai + bi))
        second.append((ar - br, ai - bi))
    return first + second


def packed(rows):
    group, part, inner = np.meshgrid(
        np.arange(rows // HALF), np.arange(2), np.arange(HALF), indexing="ij"
    )
    return (part * rows + group * HALF + inner).reshape(-1)


def trig_tables(n_az, rows):
    total = n_az * rows
    bits = n_az.bit_length() - 1
    order = packed(rows)
    tables = np.zeros((n_az, 4, 2 * rows, 2 * rows), np.float32)
    s = np.arange(rows)[None, :]
    j = np.arange(rows)[:, None]
    for p in range(n_az):
        b = bit_reverse(p, bits)
        angle = 2 * np.pi * ((s * (b + n_az * j)) % total) / total
        c, d = np.cos(angle) / math.sqrt(rows), np.sin(angle) / math.sqrt(rows)
        m = np.block([[c, d], [-d, c]])[np.ix_(order, order)]
        for at, mat in ((0, m), (2, m.T)):
            high = mat.astype(np.float32).astype(jnp.bfloat16)
            tables[p, at] = high.astype(np.float32)
            tables[p, at + 1] = mat - high.astype(np.float64)
    return tables.astype(jnp.bfloat16)


def kernel(
    n,
    ng,
    slots,
    echo_hbm,
    chirp_hbm,
    filt_hbm,
    shifts_hbm,
    tap_index_hbm,
    table_hbm,
    trig_hbm,
    out,
    echo,
    chirp,
    filt,
    shifts,
    tap_index,
    table,
    trig,
    band,
    weights,
    wide,
    partial,
    shift_wide,
    coef_wide,
    spread,
    gathering,
    send_1,
    recv_1,
    send_2,
    recv_2,
    spec,
    spec_code,
    far_code,
    halo_1,
    halo_2,
    high,
    low,
    send_3,
    recv_3,
    send_4,
    recv_4,
    local_sem,
    halo_send,
    halo_recv,
    pass_send,
    part_send,
    part_recv,
    job_send,
    job_recv,
    round_1,
    round_2,
):
    rows, cells = filt.shape[1], filt.shape[2]
    chirp_len = chirp.shape[1]
    part = cells // PARTS
    lanes = part // LANE
    groups = rows // HALF
    block = 256
    nz = 8
    me = lax.axis_index("az")
    g = lax.axis_index("rg")

    def fetch(src, dst, at):
        copy = pltpu.make_async_copy(src, dst, local_sem.at[at])
        copy.start()
        return copy

    ny = n // nz
    my_y, my_z = lax.div(me, nz), lax.rem(me, nz)
    def away(i, count):
        return count // 2 + (1 - 2 * (i % 2)) * ((i + 1) // 2)

    all_zs = [lax.rem(my_z + away(i, nz), nz) for i in range(nz)]
    barrier = pltpu.get_barrier_semaphore()

    near = [(lax.rem(my_y + d, ny), my_z) for d in (2, 1, ny - 1)]
    near = [(my_y, lax.rem(my_z + d, nz)) for d in (2, nz - 2)] + near
    near = near + [(my_y, lax.rem(my_z + d, nz)) for d in (1, nz - 1)]

    def tell(semaphore):
        for y, z in near:
            pl.semaphore_signal(semaphore, inc=1, device_id=(y * nz + z, g), device_id_type=MESH)

    tell(barrier)
    for d in (1, 2, ng - 2, ng - 1):
        pl.semaphore_signal(barrier, inc=1, device_id=(me, lax.rem(g + d, ng)), device_id_type=MESH)

    echo_copies = [
        fetch(echo_hbm.at[:, :, pl.ds(part * h, part)], echo.at[h], 6 + h) for h in range(PARTS)
    ]

    chirp_copy = fetch(chirp_hbm, chirp, 1)
    shifts_copy = fetch(shifts_hbm, shifts, 2)
    index_copy = fetch(tap_index_hbm, tap_index, 3)
    table_copy = fetch(table_hbm, table, 4)
    trig_copy = fetch(trig_hbm.at[me], trig, 5)
    filt_copy = fetch(filt_hbm, filt, 0)

    def halo_copy(src, dst, slot, d):
        return pltpu.make_async_remote_copy(
            src_ref=src,
            dst_ref=dst,
            send_sem=halo_send.at[slot],
            recv_sem=halo_recv.at[slot],
            device_id=(me, lax.rem(g - d + ng, ng)),
            device_id_type=MESH,
        )

    odd = lax.rem(g, 2) == 1

    even = lax.rem(g, 2) == 0

    def later(h):
        return h >= 1

    def sends_echo(d, h):
        far_enough = g >= d
        return far_enough & odd if d == 2 and h < PASSED else far_enough

    def pass_on(h):
        return pltpu.make_async_remote_copy(
            src_ref=wide.at[:, pl.ds(cells + part * h, part)],
            dst_ref=wide.at[:, pl.ds(2 * cells + part * h, part)],
            send_sem=pass_send.at[h],
            recv_sem=halo_recv.at[PARTS + h],
            device_id=(me, lax.rem(g - 1 + ng, ng)),
            device_id_type=MESH,
        )

    passes_on = odd & (g + 1 < ng)

    def echo_copy_of(d, h):
        return halo_copy(
            wide.at[:, pl.ds(part * h, part)],
            wide.at[:, pl.ds(d * cells + part * h, part)],
            PARTS * (d - 1) + h,
            d,
        )

    for h in range(PARTS):
        echo_copies[h].wait()
        for s in range(groups):
            at = slice(HALF * s, HALF * (s + 1))
            wide[SUB * s : SUB * (s + 1), part * h : part * (h + 1)] = jnp.concatenate(
                [echo[h, 0, at, :], echo[h, 1, at, :]], axis=0
            ).astype(BF16)
        if h == 0:
            pl.semaphore_wait(barrier, 4 + len(near))
            tell(round_1)
        pl.when(sends_echo(1, h))(echo_copy_of(1, h).start)
        if not later(h):
            pl.when(sends_echo(2, h))(echo_copy_of(2, h).start)
        else:
            pl.when(sends_echo(2, h) & even)(echo_copy_of(2, h).start)

    chirp_copy.wait()
    span = chirp_len + 2 * block
    row_id = lax.broadcasted_iota(jnp.int32, (LANE, LANE), 0)
    col_id = lax.broadcasted_iota(jnp.int32, (LANE, LANE), 1)
    mirror = (row_id + col_id == LANE - 1).astype(BF16)
    pieces = [
        jnp.dot(chirp[:, LANE * i : LANE * (i + 1)], mirror, preferred_element_type=F32)
        for i in reversed(range(chirp_len // LANE))
    ]
    edge = jnp.zeros((2, block), F32)
    base = jnp.concatenate([edge] + pieces + [edge], axis=1)
    for c in range(2):
        copies = jnp.broadcast_to(base[c : c + 1], (LANE, span))
        band[c] = pltpu.roll(copies, 1, 1, stride=1, stride_axis=0).astype(BF16)
    for a in range((chirp_len + block) // LANE):
        start = chirp_len + block - LANE * a
        for c in range(2):
            weights[LANE * a : LANE * (a + 1), block * c : block * (c + 1)] = band[
                c, :, start : start + block
            ]

    pl.semaphore_wait(round_1, len(near))
    tell(round_2)

    shifts_copy.wait()
    index_copy.wait()
    table_copy.wait()
    phases = table.shape[1]
    on_row = lax.broadcasted_iota(jnp.int32, (2 * rows, rows), 0)
    on_col = lax.broadcasted_iota(jnp.int32, (2 * rows, rows), 1)
    row_of = lax.div(on_row, SUB) * HALF + lax.rem(on_row, HALF)

    def across(values):
        return jnp.broadcast_to(values.astype(F32).reshape(1, rows), (2 * rows, rows))

    def pick(mask, values):
        return jnp.sum(jnp.where(mask, values, 0.0), axis=1, keepdims=True)

    shift_row = across(shifts[...])
    shift = pick(row_of == on_col, shift_row)
    distant = shift >= float(cells)
    rank = pick(on_col < row_of, jnp.where(shift_row >= float(cells), 1.0, 0.0))
    plain_row = lax.broadcasted_iota(jnp.int32, (rows, rows), 0)
    plain_col = lax.broadcasted_iota(jnp.int32, (rows, rows), 1)

    def upright(values):
        spread_out = jnp.broadcast_to(values.astype(F32).reshape(1, rows), (rows, rows))
        return pick(plain_row == plain_col, spread_out)

    shift_wide[...] = jnp.broadcast_to(upright(shifts[...]).astype(jnp.int32), (rows, LANE))
    phase_id = lax.broadcasted_iota(jnp.int32, (rows, phases), 1).astype(F32)
    coefs = lax.dot_general(
        jnp.where(upright(tap_index[...]) == phase_id, 1.0, 0.0),
        table[...],
        (((1,), (1,)), ((), ())),
        precision=lax.Precision.HIGHEST,
        preferred_element_type=F32,
    )
    for q in range(coef_wide.shape[0]):
        coef_wide[q] = jnp.broadcast_to(coefs[:, q : q + 1], (rows, LANE))
    from_row = lax.broadcasted_iota(jnp.int32, (2 * rows, 2 * slots), 0)
    to_slot = lax.broadcasted_iota(jnp.int32, (2 * rows, 2 * slots), 1)
    same_part = lax.rem(lax.div(from_row, HALF), 2) == lax.rem(lax.div(to_slot, HALF), 2)
    slot_of = (lax.div(to_slot, SUB) * HALF + lax.rem(to_slot, HALF)).astype(F32)
    matches = jnp.where(rank == slot_of, 1.0, 0.0) * jnp.where(same_part, 1.0, 0.0)
    matches = matches * jnp.where(distant, 1.0, 0.0)
    spread[...] = matches.astype(BF16)
    gathering[...] = matches.T.astype(BF16)

    parity = lax.rem(me, 2)

    def place(y, z):
        spot = lax.div(z, 2)
        row = SUB * (nz // 2 // lanes) * y + SUB * lax.div(spot, lanes)
        return pl.multiple_of(row, SUB), pl.multiple_of(LANE * lax.rem(spot, lanes), LANE)

    def tile(ref, p):
        row, col = place(my_y, my_z)
        return ref.at[p, pl.ds(row, SUB), pl.ds(col, LANE)]

    def other(p):
        return lax.rem(parity + p, 2)

    def scatter(src, dst, phase, p):
        job = p // JOBS

        def send(y, z):
            row, col = place(y, z)
            pltpu.make_async_remote_copy(
                src_ref=src.at[p, pl.ds(row, SUB), pl.ds(col, LANE)],
                dst_ref=dst.at[job, me],
                send_sem=part_send.at[phase, p],
                recv_sem=job_recv.at[phase, job],
                device_id=(y * nz + z, g),
                device_id_type=MESH,
            ).start()

        zs = [lax.rem(my_z + 2 * away(i, nz // 2) + other(p), nz) for i in range(nz // 2)]

        def start(k, carry):
            y = lax.rem(my_y + away(k, ny), ny)
            for z in zs:
                send(y, z)
            return carry

        lax.fori_loop(0, ny - 1, start, 0)
        for z in zs[:-1]:
            send(my_y, z)
        pl.when(other(p) == 1)(lambda: send(my_y, zs[-1]))

        @pl.when(other(p) == 0)
        def _():
            pltpu.make_async_copy(
                tile(src, p), dst.at[job, me], job_recv.at[phase, job]
            ).start()

    def gather(src, dst, phase, job):
        p = 2 * job + parity

        target = tile(dst, p)

        def send(y, z):
            q = y * nz + z
            pltpu.make_async_remote_copy(
                src_ref=src.at[job, q],
                dst_ref=target,
                send_sem=job_send.at[phase, job],
                recv_sem=part_recv.at[phase, p],
                device_id=(q, g),
                device_id_type=MESH,
            ).start()

        def start(k, carry):
            y = lax.rem(my_y + away(k, ny), ny)
            for z in all_zs:
                send(y, z)
            return carry

        lax.fori_loop(0, ny - 1, start, 0)
        for z in all_zs[:-1]:
            send(my_y, z)
        pltpu.make_async_copy(src.at[job, me], target, part_recv.at[phase, p]).start()

    def scattered(dst, phase, job):
        pltpu.make_async_copy(dst.at[job], dst.at[job], job_recv.at[phase, job]).wait()

    def gathered(dst, phase, p):
        pltpu.make_async_copy(dst.at[p], dst.at[p], part_recv.at[phase, p]).wait()

    def transform(fft, src, dst, h):
        xs = []
        for p in range(n):
            value = decode(src[h, p])
            xs.append((value[:HALF], value[HALF:]))
        for p, (re, im) in enumerate(fft(xs)):
            dst[h, p] = encode(jnp.concatenate([re, im], axis=0) * (1.0 / math.sqrt(n)))

    def compress_near(h):
        reach = 2 * cells - part * h
        partial[h] = jnp.dot(
            wide[:, part * h : 2 * cells], weights[:reach, :], preferred_element_type=F32
        )

    def compress(h):
        reach = 2 * cells - part * h
        product = partial[h] + jnp.dot(
            wide[:, 2 * cells : part * h + chirp_len + block],
            weights[reach:, :],
            preferred_element_type=F32,
        )
        piece = product.reshape(groups, 2, HALF, 2 * block)
        real = piece[:, 0, :, :block] - piece[:, 1, :, block:]
        imag = piece[:, 0, :, block:] + piece[:, 1, :, :block]
        send_1[h] = encode(jnp.concatenate([real, imag], axis=1).reshape(2 * rows, block))

    def echo_arrived(d, h):
        pl.when(g + d < ng)(echo_copy_of(d, h).wait_recv)

        @pl.when(g + d >= ng)
        def _():
            start = d * cells + part * h
            wide[:, start : start + part] = jnp.zeros((2 * rows, part), BF16)

    for h in range(PARTS):
        echo_arrived(1, h)
        if h < PASSED:
            pl.when(passes_on)(pass_on(h).start)
        if h == 0:
            for i in range(PARTS):
                if later(i):
                    pl.when(sends_echo(2, i) & odd)(echo_copy_of(2, i).start)
    pl.semaphore_wait(round_2, len(near))
    for h in range(PARTS):
        compress_near(h)
        echo_arrived(2, h)
        compress(h)
        scatter(send_1, recv_1, 0, h)

    for job in range(JOBS):
        scattered(recv_1, 0, job)
        transform(fft_forward, recv_1, send_2, job)
        gather(send_2, recv_2, 0, job)

    def times(at, upper, lower):
        return jnp.dot(
            jnp.concatenate([trig[at], trig[at + 1], trig[at]], axis=1),
            jnp.concatenate([upper, upper, lower], axis=0),
            preferred_element_type=F32,
        )

    def split(value):
        upper = value.astype(BF16)
        return upper, (value - upper.astype(F32)).astype(BF16)

    def spec_copy_of(d, h):
        src, dst = ((spec_code, halo_1), (far_code, halo_2))[d - 1]
        return halo_copy(src.at[h], dst.at[h], 2 * PARTS + PARTS * (d - 1) + h, d)

    trig_copy.wait()
    for h in range(PARTS):
        gathered(recv_2, 0, h)
        spectrum = times(0, *split(decode(recv_2[h])))
        code = encode(spectrum)
        spec_code[h] = code
        pl.when(g >= 1)(spec_copy_of(1, h).start)
        far_code[h] = jnp.dot(gathering[...], code, preferred_element_type=F32).astype(BF16)
        pl.when(g >= 2)(spec_copy_of(2, h).start)
        spec[:, part * h : part * (h + 1)] = spectrum

    def spec_arrived(d, h):
        dst = (halo_1, halo_2)[d - 1]
        pl.when(g + d < ng)(spec_copy_of(d, h).wait_recv)

        @pl.when(g + d >= ng)
        def _():
            dst[h] = jnp.zeros(dst.shape[1:], BF16)

        start = d * cells + part * h
        if d == 1:
            value = halo_1[h]
        else:
            value = jnp.dot(spread[...], halo_2[h], preferred_element_type=F32)
        spec[:, start : start + part] = decode(value)


    lane = lax.broadcasted_iota(jnp.int32, (HALF, LANE), 1)
    block_tiles = cells // LANE
    reach = cells // 2
    lanes_out = reach // LANE

    def ahead(xs, by):
        moved = [pltpu.roll(x, LANE - by, 1) for x in xs]
        kept = lane < LANE - by
        return [jnp.where(kept, a, b) for a, b in zip(moved, moved[1:])] + [moved[-1]]

    def migrate(h):
        start = reach * h

        def row_group(j):
            at = pl.multiple_of(SUB * j, SUB)
            own = pl.multiple_of(HALF * j, HALF)
            shift = shift_wide[pl.ds(own, HALF), :]
            distant = shift >= cells
            rest = jnp.where(distant, shift - cells, shift)
            fine = rest & (LANE - 1)
            turned = lane + fine
            inside = turned < LANE
            turned = jnp.where(inside, turned, turned - LANE)
            totals = []
            for c in range(2):
                row = pl.ds(pl.multiple_of(at + HALF * c, HALF), HALF)

                def load(t):
                    return spec[row, start + LANE * t : start + LANE * (t + 1)]

                count = lanes_out + block_tiles
                cur = [
                    jnp.where(distant, load(t + block_tiles), load(t)) for t in range(count)
                ]
                step = block_tiles // 2
                while step >= 1:
                    bit = (rest & (step * LANE)) != 0
                    width = lanes_out + step + 1
                    cur = [
                        jnp.where(bit, cur[min(t + step, count - 1)], cur[t]) for t in range(width)
                    ]
                    count = width
                    step //= 2
                cur = [jnp.take_along_axis(x, turned, axis=1) for x in cur]
                cur = [jnp.where(inside, cur[t], cur[t + 1]) for t in range(lanes_out + 1)]
                weight = [coef_wide[q, pl.ds(own, HALF), :] for q in range(8)]
                four = ahead(cur, 4)
                pair = [
                    [weight[q] * x + weight[q + 4] * y for x, y in zip(cur, four)]
                    for q in range(4)
                ]
                even = [x + y for x, y in zip(pair[0], ahead(pair[2], 2))]
                odd = [x + y for x, y in zip(pair[1], ahead(pair[3], 2))]
                total = [x + y for x, y in zip(even, ahead(odd, 1))]
                totals.append(total)
            for t in range(lanes_out):
                col = slice(start + LANE * t, start + LANE * (t + 1))
                fr = filt[0, pl.ds(own, HALF), col]
                fi = filt[1, pl.ds(own, HALF), col]
                x, y = totals[0][t], totals[1][t]
                both = jnp.concatenate([x * fr - y * fi, x * fi + y * fr], axis=0)
                upper, lower = split(both)
                high[pl.ds(at, SUB), col] = upper
                low[pl.ds(at, SUB), col] = lower

        def some(j, carry):
            for u in range(UNROLL):
                row_group(UNROLL * j + u)
            return carry

        lax.fori_loop(0, groups // UNROLL, some, 0)

    for h in range(PARTS):
        spec_arrived(1, h)
    filt_copy.wait()
    for h in range(PARTS):
        if h % 2 == 0:
            spec_arrived(2, h)
            spec_arrived(2, h + 1)
            migrate(h // 2)
        col = slice(part * h, part * (h + 1))
        send_3[h] = encode(times(2, high[:, col], low[:, col]))
        scatter(send_3, recv_3, 1, h)

    for job in range(JOBS):
        scattered(recv_3, 1, job)
        transform(fft_inverse, recv_3, send_4, job)
        gather(send_4, recv_4, 1, job)
    for h in range(PARTS):
        gathered(recv_4, 1, h)
        for s in range(groups):
            value = decode(recv_4[h, SUB * s : SUB * (s + 1), :])
            for c in range(2):
                out[c, HALF * s : HALF * (s + 1), part * h : part * (h + 1)] = value[
                    HALF * c : HALF * (c + 1)
                ]

    for h in range(PASSED):
        pl.when(passes_on)(pass_on(h).wait_send)
    for d in (1, 2):
        for h in range(PARTS):
            pl.when(sends_echo(d, h))(echo_copy_of(d, h).wait_send)
            pl.when(g >= d)(spec_copy_of(d, h).wait_send)
    for phase in range(2):
        for job in range(JOBS):
            sent = send_2.at[0, pl.ds(0, n - 1)]
            pltpu.make_async_copy(sent, sent, job_send.at[phase, job]).wait()
        for p in range(PARTS):
            for same in (0, 1):
                sent = send_2.at[0, pl.ds(0, n // 2 - 1 + same)]
                pl.when(other(p) == same)(
                    pltpu.make_async_copy(sent, sent, part_send.at[phase, p]).wait
                )


def solution(mesh):
    n, ng = mesh.shape["az"], mesh.shape["rg"]

    def local(echo_field, range_chirp, azimuth_filter, shifts, tap_index, taps_table):
        rows, cells = echo_field.shape[1], echo_field.shape[2]
        chirp_len = range_chirp.shape[1]
        phases, taps = taps_table.shape
        block = 256
        slots = rows // 2
        part = cells // PARTS
        trig = jnp.asarray(trig_tables(n, rows))
        stack = (2, rows, cells)
        flat = (PARTS, 2 * rows, part)
        tiles = (JOBS, n, SUB, LANE)
        hbm = pl.BlockSpec(memory_space=pltpu.HBM)
        return pl.pallas_call(
            functools.partial(kernel, n, ng, slots),
            out_shape=pltpu.VMEM(stack, F32),
            in_specs=[hbm] * 7,
            out_specs=pl.BlockSpec(memory_space=pltpu.VMEM),
            scratch_shapes=[
                pltpu.VMEM((PARTS, 2, rows, part), F32),
                pltpu.VMEM((2, chirp_len), BF16),
                pltpu.VMEM(stack, F32),
                pltpu.VMEM((rows,), jnp.int32),
                pltpu.VMEM((rows,), jnp.int32),
                pltpu.VMEM((taps, phases), F32),
                pltpu.VMEM((4, 2 * rows, 2 * rows), BF16),
                pltpu.VMEM((2, LANE, chirp_len + 2 * block), BF16),
                pltpu.VMEM((chirp_len + block, 2 * block), BF16),
                pltpu.VMEM((2 * rows, 3 * cells), BF16),
                pltpu.VMEM((PARTS, 2 * rows, 2 * block), F32),
                pltpu.VMEM((rows, LANE), jnp.int32),
                pltpu.VMEM((taps, rows, LANE), F32),
                pltpu.VMEM((2 * rows, 2 * slots), BF16),
                pltpu.VMEM((2 * slots, 2 * rows), BF16),
                pltpu.VMEM(flat, BF16),
                pltpu.VMEM(tiles, BF16),
                pltpu.VMEM(tiles, BF16),
                pltpu.VMEM(flat, BF16),
                pltpu.VMEM((2 * rows, 3 * cells), F32),
                pltpu.VMEM(flat, BF16),
                pltpu.VMEM((PARTS, 2 * slots, part), BF16),
                pltpu.VMEM(flat, BF16),
                pltpu.VMEM((PARTS, 2 * slots, part), BF16),
                pltpu.VMEM((2 * rows, cells), BF16),
                pltpu.VMEM((2 * rows, cells), BF16),
                pltpu.VMEM(flat, BF16),
                pltpu.VMEM(tiles, BF16),
                pltpu.VMEM(tiles, BF16),
                pltpu.VMEM(flat, BF16),
                pltpu.SemaphoreType.DMA((6 + PARTS,)),
                pltpu.SemaphoreType.DMA((4 * PARTS,)),
                pltpu.SemaphoreType.DMA((4 * PARTS,)),
                pltpu.SemaphoreType.DMA((PASSED,)),
                pltpu.SemaphoreType.DMA((2, PARTS)),
                pltpu.SemaphoreType.DMA((2, PARTS)),
                pltpu.SemaphoreType.DMA((2, JOBS)),
                pltpu.SemaphoreType.DMA((2, JOBS)),
                pltpu.SemaphoreType.REGULAR,
                pltpu.SemaphoreType.REGULAR,
            ],
            compiler_params=pltpu.CompilerParams(
                collective_id=0, has_side_effects=True, vmem_limit_bytes=48 * 1024 * 1024
            ),
            cost_estimate=pl.CostEstimate(
                flops=1_600_000_000, bytes_accessed=2_000_000, transcendentals=0
            ),
        )(
            *(
                pltpu.with_memory_space_constraint(x, pltpu.HBM)
                for x in (
                    echo_field,
                    range_chirp,
                    azimuth_filter,
                    shifts,
                    tap_index,
                    taps_table.T,
                    trig,
                )
            )
        )

    placed = (P(None, "az", "rg"), P(), P(None, "az", "rg"), P("az"), P("az"), P())
    return jax.shard_map(
        local, mesh=mesh, in_specs=placed, out_specs=P(None, "az", "rg"), check_vma=False
    )
```

```python
import functools
import math

import jax
import jax.numpy as jnp
import numpy as np
from jax import lax
from jax.experimental import pallas as pl
from jax.experimental.pallas import tpu as pltpu
from jax.sharding import PartitionSpec as P

MESH = pl.DeviceIdType.MESH
F32 = jnp.float32
BF16 = jnp.bfloat16
LANE = 128
SUB = 16
HALF = 8
PARTS = 4
JOBS = 2
PASSED = 3
UNROLL = 4


def encode(x):
    return (x * jnp.abs(x)).astype(BF16)


def decode(code):
    c = code.astype(F32)
    return c * lax.rsqrt(jnp.maximum(jnp.abs(c), 1e-37))


def bit_reverse(value, bits):
    result = 0
    for position in range(bits):
        result += ((value >> position) & 1) << (bits - 1 - position)
    return result


def turn(pair, k, n, sign):
    re, im = pair
    if k == 0:
        return re, im
    if 4 * k == n:
        return (-im, re) if sign > 0 else (im, -re)
    c = math.cos(2 * math.pi * k / n)
    s = sign * math.sin(2 * math.pi * k / n)
    if 8 * k == n:
        return ((re - im) * c, (re + im) * c) if sign > 0 else ((re + im) * c, (im - re) * c)
    if 8 * k == 3 * n:
        h = -c
        return (-(re + im) * h, (re - im) * h) if sign > 0 else ((im - re) * h, -(re + im) * h)
    return re * c - im * s, re * s + im * c


def fft_forward(xs):
    n = len(xs)
    if n == 1:
        return xs
    half = n // 2
    low, high = [], []
    for k in range(half):
        (ar, ai), (br, bi) = xs[k], xs[k + half]
        low.append((ar + br, ai + bi))
        high.append(turn((ar - br, ai - bi), k, n, -1))
    return fft_forward(low) + fft_forward(high)


def fft_inverse(xs):
    n = len(xs)
    if n == 1:
        return xs
    half = n // 2
    low = fft_inverse(xs[:half])
    high = fft_inverse(xs[half:])
    first, second = [], []
    for k in range(half):
        ar, ai = low[k]
        br, bi = turn(high[k], k, n, 1)
        first.append((ar + br, ai + bi))
        second.append((ar - br, ai - bi))
    return first + second


def packed(rows):
    group, part, inner = np.meshgrid(
        np.arange(rows // HALF), np.arange(2), np.arange(HALF), indexing="ij"
    )
    return (part * rows + group * HALF + inner).reshape(-1)


def trig_tables(n_az, rows):
    total = n_az * rows
    bits = n_az.bit_length() - 1
    order = packed(rows)
    tables = np.zeros((n_az, 4, 2 * rows, 2 * rows), np.float32)
    s = np.arange(rows)[None, :]
    j = np.arange(rows)[:, None]
    for p in range(n_az):
        b = bit_reverse(p, bits)
        angle = 2 * np.pi * ((s * (b + n_az * j)) % total) / total
        c, d = np.cos(angle) / math.sqrt(rows), np.sin(angle) / math.sqrt(rows)
        m = np.block([[c, d], [-d, c]])[np.ix_(order, order)]
        for at, mat in ((0, m), (2, m.T)):
            high = mat.astype(np.float32).astype(jnp.bfloat16)
            tables[p, at] = high.astype(np.float32)
            tables[p, at + 1] = mat - high.astype(np.float64)
    return tables.astype(jnp.bfloat16)


def kernel(
    n,
    ng,
    slots,
    echo_hbm,
    chirp_hbm,
    filt_hbm,
    shifts_hbm,
    tap_index_hbm,
    table_hbm,
    trig_hbm,
    out,
    echo,
    chirp,
    filt,
    shifts,
    tap_index,
    table,
    trig,
    band,
    weights,
    wide,
    partial,
    shift_wide,
    coef_wide,
    spread,
    gathering,
    send_1,
    recv_1,
    send_2,
    recv_2,
    spec,
    spec_code,
    far_code,
    halo_1,
    halo_2,
    high,
    low,
    send_3,
    recv_3,
    send_4,
    recv_4,
    local_sem,
    halo_send,
    halo_recv,
    pass_send,
    part_send,
    part_recv,
    job_send,
    job_recv,
    round_1,
    round_2,
):
    rows, cells = filt.shape[1], filt.shape[2]
    chirp_len = chirp.shape[1]
    part = cells // PARTS
    lanes = part // LANE
    groups = rows // HALF
    block = 256
    nz = 8
    me = lax.axis_index("az")
    g = lax.axis_index("rg")

    def fetch(src, dst, at):
        copy = pltpu.make_async_copy(src, dst, local_sem.at[at])
        copy.start()
        return copy

    ny = n // nz
    my_y, my_z = lax.div(me, nz), lax.rem(me, nz)
    def away(i, count):
        return count // 2 + (1 - 2 * (i % 2)) * ((i + 1) // 2)

    all_zs = [lax.rem(my_z + away(i, nz), nz) for i in range(nz)]
    barrier = pltpu.get_barrier_semaphore()

    near = [(lax.rem(my_y + d, ny), my_z) for d in (2, 1, ny - 1)]
    near = [(my_y, lax.rem(my_z + d, nz)) for d in (2, nz - 2)] + near
    near = near + [(my_y, lax.rem(my_z + d, nz)) for d in (1, nz - 1)]

    def tell(semaphore):
        for y, z in near:
            pl.semaphore_signal(semaphore, inc=1, device_id=(y * nz + z, g), device_id_type=MESH)

    tell(barrier)
    for d in (1, 2, ng - 2, ng - 1):
        pl.semaphore_signal(barrier, inc=1, device_id=(me, lax.rem(g + d, ng)), device_id_type=MESH)

    echo_copies = [
        fetch(echo_hbm.at[:, :, pl.ds(part * h, part)], echo.at[h], 6 + h) for h in range(PARTS)
    ]

    chirp_copy = fetch(chirp_hbm, chirp, 1)
    shifts_copy = fetch(shifts_hbm, shifts, 2)
    index_copy = fetch(tap_index_hbm, tap_index, 3)
    table_copy = fetch(table_hbm, table, 4)
    trig_copy = fetch(trig_hbm.at[me], trig, 5)
    filt_copy = fetch(filt_hbm, filt, 0)

    def halo_copy(src, dst, slot, d):
        return pltpu.make_async_remote_copy(
            src_ref=src,
            dst_ref=dst,
            send_sem=halo_send.at[slot],
            recv_sem=halo_recv.at[slot],
            device_id=(me, lax.rem(g - d + ng, ng)),
            device_id_type=MESH,
        )

    odd = lax.rem(g, 2) == 1

    even = lax.rem(g, 2) == 0

    def later(h):
        return h >= 1

    def sends_echo(d, h):
        far_enough = g >= d
        return far_enough & odd if d == 2 and h < PASSED else far_enough

    def pass_on(h):
        return pltpu.make_async_remote_copy(
            src_ref=wide.at[:, pl.ds(cells + part * h, part)],
            dst_ref=wide.at[:, pl.ds(2 * cells + part * h, part)],
            send_sem=pass_send.at[h],
            recv_sem=halo_recv.at[PARTS + h],
            device_id=(me, lax.rem(g - 1 + ng, ng)),
            device_id_type=MESH,
        )

    passes_on = odd & (g + 1 < ng)

    def echo_copy_of(d, h):
        return halo_copy(
            wide.at[:, pl.ds(part * h, part)],
            wide.at[:, pl.ds(d * cells + part * h, part)],
            PARTS * (d - 1) + h,
            d,
        )

    for h in range(PARTS):
        echo_copies[h].wait()
        for s in range(groups):
            at = slice(HALF * s, HALF * (s + 1))
            wide[SUB * s : SUB * (s + 1), part * h : part * (h + 1)] = jnp.concatenate(
                [echo[h, 0, at, :], echo[h, 1, at, :]], axis=0
            ).astype(BF16)
        if h == 0:
            pl.semaphore_wait(barrier, 4 + len(near))
        pl.when(sends_echo(1, h))(echo_copy_of(1, h).start)
        if not later(h):
            pl.when(sends_echo(2, h))(echo_copy_of(2, h).start)
        else:
            pl.when(sends_echo(2, h) & even)(echo_copy_of(2, h).start)
        if h == 1:
            tell(round_1)

    chirp_copy.wait()
    span = chirp_len + 2 * block
    row_id = lax.broadcasted_iota(jnp.int32, (LANE, LANE), 0)
    col_id = lax.broadcasted_iota(jnp.int32, (LANE, LANE), 1)
    mirror = (row_id + col_id == LANE - 1).astype(BF16)
    pieces = [
        jnp.dot(chirp[:, LANE * i : LANE * (i + 1)], mirror, preferred_element_type=F32)
        for i in reversed(range(chirp_len // LANE))
    ]
    edge = jnp.zeros((2, block), F32)
    base = jnp.concatenate([edge] + pieces + [edge], axis=1)
    for c in range(2):
        copies = jnp.broadcast_to(base[c : c + 1], (LANE, span))
        band[c] = pltpu.roll(copies, 1, 1, stride=1, stride_axis=0).astype(BF16)
    for a in range((chirp_len + block) // LANE):
        start = chirp_len + block - LANE * a
        for c in range(2):
            weights[LANE * a : LANE * (a + 1), block * c : block * (c + 1)] = band[
                c, :, start : start + block
            ]

    pl.semaphore_wait(round_1, len(near))
    tell(round_2)

    shifts_copy.wait()
    index_copy.wait()
    table_copy.wait()
    phases = table.shape[1]
    on_row = lax.broadcasted_iota(jnp.int32, (2 * rows, rows), 0)
    on_col = lax.broadcasted_iota(jnp.int32, (2 * rows, rows), 1)
    row_of = lax.div(on_row, SUB) * HALF + lax.rem(on_row, HALF)

    def across(values):
        return jnp.broadcast_to(values.astype(F32).reshape(1, rows), (2 * rows, rows))

    def pick(mask, values):
        return jnp.sum(jnp.where(mask, values, 0.0), axis=1, keepdims=True)

    shift_row = across(shifts[...])
    shift = pick(row_of == on_col, shift_row)
    distant = shift >= float(cells)
    rank = pick(on_col < row_of, jnp.where(shift_row >= float(cells), 1.0, 0.0))
    plain_row = lax.broadcasted_iota(jnp.int32, (rows, rows), 0)
    plain_col = lax.broadcasted_iota(jnp.int32, (rows, rows), 1)

    def upright(values):
        spread_out = jnp.broadcast_to(values.astype(F32).reshape(1, rows), (rows, rows))
        return pick(plain_row == plain_col, spread_out)

    shift_wide[...] = jnp.broadcast_to(upright(shifts[...]).astype(jnp.int32), (rows, LANE))
    phase_id = lax.broadcasted_iota(jnp.int32, (rows, phases), 1).astype(F32)
    coefs = lax.dot_general(
        jnp.where(upright(tap_index[...]) == phase_id, 1.0, 0.0),
        table[...],
        (((1,), (1,)), ((), ())),
        precision=lax.Precision.HIGHEST,
        preferred_element_type=F32,
    )
    for q in range(coef_wide.shape[0]):
        coef_wide[q] = jnp.broadcast_to(coefs[:, q : q + 1], (rows, LANE))
    from_row = lax.broadcasted_iota(jnp.int32, (2 * rows, 2 * slots), 0)
    to_slot = lax.broadcasted_iota(jnp.int32, (2 * rows, 2 * slots), 1)
    same_part = lax.rem(lax.div(from_row, HALF), 2) == lax.rem(lax.div(to_slot, HALF), 2)
    slot_of = (lax.div(to_slot, SUB) * HALF + lax.rem(to_slot, HALF)).astype(F32)
    matches = jnp.where(rank == slot_of, 1.0, 0.0) * jnp.where(same_part, 1.0, 0.0)
    matches = matches * jnp.where(distant, 1.0, 0.0)
    spread[...] = matches.astype(BF16)
    gathering[...] = matches.T.astype(BF16)

    parity = lax.rem(me, 2)

    def place(y, z):
        spot = lax.div(z, 2)
        row = SUB * (nz // 2 // lanes) * y + SUB * lax.div(spot, lanes)
        return pl.multiple_of(row, SUB), pl.multiple_of(LANE * lax.rem(spot, lanes), LANE)

    def tile(ref, p):
        row, col = place(my_y, my_z)
        return ref.at[p, pl.ds(row, SUB), pl.ds(col, LANE)]

    def other(p):
        return lax.rem(parity + p, 2)

    def scatter(src, dst, phase, p):
        job = p // JOBS

        def send(y, z):
            row, col = place(y, z)
            pltpu.make_async_remote_copy(
                src_ref=src.at[p, pl.ds(row, SUB), pl.ds(col, LANE)],
                dst_ref=dst.at[job, me],
                send_sem=part_send.at[phase, p],
                recv_sem=job_recv.at[phase, job],
                device_id=(y * nz + z, g),
                device_id_type=MESH,
            ).start()

        zs = [lax.rem(my_z + 2 * away(i, nz // 2) + other(p), nz) for i in range(nz // 2)]

        def start(k, carry):
            y = lax.rem(my_y + away(k, ny), ny)
            for z in zs:
                send(y, z)
            return carry

        lax.fori_loop(0, ny - 1, start, 0)
        for z in zs[:-1]:
            send(my_y, z)
        pl.when(other(p) == 1)(lambda: send(my_y, zs[-1]))

        @pl.when(other(p) == 0)
        def _():
            pltpu.make_async_copy(
                tile(src, p), dst.at[job, me], job_recv.at[phase, job]
            ).start()

    def gather(src, dst, phase, job):
        p = 2 * job + parity

        target = tile(dst, p)

        def send(y, z):
            q = y * nz + z
            pltpu.make_async_remote_copy(
                src_ref=src.at[job, q],
                dst_ref=target,
                send_sem=job_send.at[phase, job],
                recv_sem=part_recv.at[phase, p],
                device_id=(q, g),
                device_id_type=MESH,
            ).start()

        def start(k, carry):
            y = lax.rem(my_y + away(k, ny), ny)
            for z in all_zs:
                send(y, z)
            return carry

        lax.fori_loop(0, ny - 1, start, 0)
        for z in all_zs[:-1]:
            send(my_y, z)
        pltpu.make_async_copy(src.at[job, me], target, part_recv.at[phase, p]).start()

    def scattered(dst, phase, job):
        pltpu.make_async_copy(dst.at[job], dst.at[job], job_recv.at[phase, job]).wait()

    def gathered(dst, phase, p):
        pltpu.make_async_copy(dst.at[p], dst.at[p], part_recv.at[phase, p]).wait()

    def transform(fft, src, dst, h):
        xs = []
        for p in range(n):
            value = decode(src[h, p])
            xs.append((value[:HALF], value[HALF:]))
        for p, (re, im) in enumerate(fft(xs)):
            dst[h, p] = encode(jnp.concatenate([re, im], axis=0) * (1.0 / math.sqrt(n)))

    def compress_near(h):
        reach = 2 * cells - part * h
        partial[h] = jnp.dot(
            wide[:, part * h : 2 * cells], weights[:reach, :], preferred_element_type=F32
        )

    def compress(h):
        reach = 2 * cells - part * h
        product = partial[h] + jnp.dot(
            wide[:, 2 * cells : part * h + chirp_len + block],
            weights[reach:, :],
            preferred_element_type=F32,
        )
        piece = product.reshape(groups, 2, HALF, 2 * block)
        real = piece[:, 0, :, :block] - piece[:, 1, :, block:]
        imag = piece[:, 0, :, block:] + piece[:, 1, :, :block]
        send_1[h] = encode(jnp.concatenate([real, imag], axis=1).reshape(2 * rows, block))

    def echo_arrived(d, h):
        pl.when(g + d < ng)(echo_copy_of(d, h).wait_recv)

        @pl.when(g + d >= ng)
        def _():
            start = d * cells + part * h
            wide[:, start : start + part] = jnp.zeros((2 * rows, part), BF16)

    for h in range(PARTS):
        echo_arrived(1, h)
        if h < PASSED:
            pl.when(passes_on)(pass_on(h).start)
        if h == 0:
            for i in range(PARTS):
                if later(i):
                    pl.when(sends_echo(2, i) & odd)(echo_copy_of(2, i).start)
    pl.semaphore_wait(round_2, len(near))
    for h in range(PARTS):
        compress_near(h)
        echo_arrived(2, h)
        compress(h)
        scatter(send_1, recv_1, 0, h)

    for job in range(JOBS):
        scattered(recv_1, 0, job)
        transform(fft_forward, recv_1, send_2, job)
        gather(send_2, recv_2, 0, job)

    def times(at, upper, lower):
        return jnp.dot(
            jnp.concatenate([trig[at], trig[at + 1], trig[at]], axis=1),
            jnp.concatenate([upper, upper, lower], axis=0),
            preferred_element_type=F32,
        )

    def split(value):
        upper = value.astype(BF16)
        return upper, (value - upper.astype(F32)).astype(BF16)

    def spec_copy_of(d, h):
        src, dst = ((spec_code, halo_1), (far_code, halo_2))[d - 1]
        return halo_copy(src.at[h], dst.at[h], 2 * PARTS + PARTS * (d - 1) + h, d)

    trig_copy.wait()
    for h in range(PARTS):
        gathered(recv_2, 0, h)
        spectrum = times(0, *split(decode(recv_2[h])))
        code = encode(spectrum)
        spec_code[h] = code
        pl.when(g >= 1)(spec_copy_of(1, h).start)
        far_code[h] = jnp.dot(gathering[...], code, preferred_element_type=F32).astype(BF16)
        pl.when(g >= 2)(spec_copy_of(2, h).start)
        spec[:, part * h : part * (h + 1)] = spectrum

    def spec_arrived(d, h):
        dst = (halo_1, halo_2)[d - 1]
        pl.when(g + d < ng)(spec_copy_of(d, h).wait_recv)

        @pl.when(g + d >= ng)
        def _():
            dst[h] = jnp.zeros(dst.shape[1:], BF16)

        start = d * cells + part * h
        if d == 1:
            value = halo_1[h]
        else:
            value = jnp.dot(spread[...], halo_2[h], preferred_element_type=F32)
        spec[:, start : start + part] = decode(value)


    lane = lax.broadcasted_iota(jnp.int32, (HALF, LANE), 1)
    block_tiles = cells // LANE
    reach = cells // 2
    lanes_out = reach // LANE

    def ahead(xs, by):
        moved = [pltpu.roll(x, LANE - by, 1) for x in xs]
        kept = lane < LANE - by
        return [jnp.where(kept, a, b) for a, b in zip(moved, moved[1:])] + [moved[-1]]

    def migrate(h):
        start = reach * h

        def row_group(j):
            at = pl.multiple_of(SUB * j, SUB)
            own = pl.multiple_of(HALF * j, HALF)
            shift = shift_wide[pl.ds(own, HALF), :]
            distant = shift >= cells
            rest = jnp.where(distant, shift - cells, shift)
            fine = rest & (LANE - 1)
            turned = lane + fine
            inside = turned < LANE
            turned = jnp.where(inside, turned, turned - LANE)
            totals = []
            for c in range(2):
                row = pl.ds(pl.multiple_of(at + HALF * c, HALF), HALF)

                def load(t):
                    return spec[row, start + LANE * t : start + LANE * (t + 1)]

                count = lanes_out + block_tiles
                cur = [
                    jnp.where(distant, load(t + block_tiles), load(t)) for t in range(count)
                ]
                step = block_tiles // 2
                while step >= 1:
                    bit = (rest & (step * LANE)) != 0
                    width = lanes_out + step + 1
                    cur = [
                        jnp.where(bit, cur[min(t + step, count - 1)], cur[t]) for t in range(width)
                    ]
                    count = width
                    step //= 2
                cur = [jnp.take_along_axis(x, turned, axis=1) for x in cur]
                cur = [jnp.where(inside, cur[t], cur[t + 1]) for t in range(lanes_out + 1)]
                weight = [coef_wide[q, pl.ds(own, HALF), :] for q in range(8)]
                four = ahead(cur, 4)
                pair = [
                    [weight[q] * x + weight[q + 4] * y for x, y in zip(cur, four)]
                    for q in range(4)
                ]
                even = [x + y for x, y in zip(pair[0], ahead(pair[2], 2))]
                odd = [x + y for x, y in zip(pair[1], ahead(pair[3], 2))]
                total = [x + y for x, y in zip(even, ahead(odd, 1))]
                totals.append(total)
            for t in range(lanes_out):
                col = slice(start + LANE * t, start + LANE * (t + 1))
                fr = filt[0, pl.ds(own, HALF), col]
                fi = filt[1, pl.ds(own, HALF), col]
                x, y = totals[0][t], totals[1][t]
                both = jnp.concatenate([x * fr - y * fi, x * fi + y * fr], axis=0)
                upper, lower = split(both)
                high[pl.ds(at, SUB), col] = upper
                low[pl.ds(at, SUB), col] = lower

        def some(j, carry):
            for u in range(UNROLL):
                row_group(UNROLL * j + u)
            return carry

        lax.fori_loop(0, groups // UNROLL, some, 0)

    for h in range(PARTS):
        spec_arrived(1, h)
    filt_copy.wait()
    for h in range(PARTS):
        if h % 2 == 0:
            spec_arrived(2, h)
            spec_arrived(2, h + 1)
            migrate(h // 2)
        col = slice(part * h, part * (h + 1))
        send_3[h] = encode(times(2, high[:, col], low[:, col]))
        scatter(send_3, recv_3, 1, h)

    for job in range(JOBS):
        scattered(recv_3, 1, job)
        transform(fft_inverse, recv_3, send_4, job)
        gather(send_4, recv_4, 1, job)
    for h in range(PARTS):
        gathered(recv_4, 1, h)
        for s in range(groups):
            value = decode(recv_4[h, SUB * s : SUB * (s + 1), :])
            for c in range(2):
                out[c, HALF * s : HALF * (s + 1), part * h : part * (h + 1)] = value[
                    HALF * c : HALF * (c + 1)
                ]

    for h in range(PASSED):
        pl.when(passes_on)(pass_on(h).wait_send)
    for d in (1, 2):
        for h in range(PARTS):
            pl.when(sends_echo(d, h))(echo_copy_of(d, h).wait_send)
            pl.when(g >= d)(spec_copy_of(d, h).wait_send)
    for phase in range(2):
        for job in range(JOBS):
            sent = send_2.at[0, pl.ds(0, n - 1)]
            pltpu.make_async_copy(sent, sent, job_send.at[phase, job]).wait()
        for p in range(PARTS):
            for same in (0, 1):
                sent = send_2.at[0, pl.ds(0, n // 2 - 1 + same)]
                pl.when(other(p) == same)(
                    pltpu.make_async_copy(sent, sent, part_send.at[phase, p]).wait
                )


def solution(mesh):
    n, ng = mesh.shape["az"], mesh.shape["rg"]

    def local(echo_field, range_chirp, azimuth_filter, shifts, tap_index, taps_table):
        rows, cells = echo_field.shape[1], echo_field.shape[2]
        chirp_len = range_chirp.shape[1]
        phases, taps = taps_table.shape
        block = 256
        slots = rows // 2
        part = cells // PARTS
        trig = jnp.asarray(trig_tables(n, rows))
        stack = (2, rows, cells)
        flat = (PARTS, 2 * rows, part)
        tiles = (JOBS, n, SUB, LANE)
        hbm = pl.BlockSpec(memory_space=pltpu.HBM)
        return pl.pallas_call(
            functools.partial(kernel, n, ng, slots),
            out_shape=pltpu.VMEM(stack, F32),
            in_specs=[hbm] * 7,
            out_specs=pl.BlockSpec(memory_space=pltpu.VMEM),
            scratch_shapes=[
                pltpu.VMEM((PARTS, 2, rows, part), F32),
                pltpu.VMEM((2, chirp_len), BF16),
                pltpu.VMEM(stack, F32),
                pltpu.VMEM((rows,), jnp.int32),
                pltpu.VMEM((rows,), jnp.int32),
                pltpu.VMEM((taps, phases), F32),
                pltpu.VMEM((4, 2 * rows, 2 * rows), BF16),
                pltpu.VMEM((2, LANE, chirp_len + 2 * block), BF16),
                pltpu.VMEM((chirp_len + block, 2 * block), BF16),
                pltpu.VMEM((2 * rows, 3 * cells), BF16),
                pltpu.VMEM((PARTS, 2 * rows, 2 * block), F32),
                pltpu.VMEM((rows, LANE), jnp.int32),
                pltpu.VMEM((taps, rows, LANE), F32),
                pltpu.VMEM((2 * rows, 2 * slots), BF16),
                pltpu.VMEM((2 * slots, 2 * rows), BF16),
                pltpu.VMEM(flat, BF16),
                pltpu.VMEM(tiles, BF16),
                pltpu.VMEM(tiles, BF16),
                pltpu.VMEM(flat, BF16),
                pltpu.VMEM((2 * rows, 3 * cells), F32),
                pltpu.VMEM(flat, BF16),
                pltpu.VMEM((PARTS, 2 * slots, part), BF16),
                pltpu.VMEM(flat, BF16),
                pltpu.VMEM((PARTS, 2 * slots, part), BF16),
                pltpu.VMEM((2 * rows, cells), BF16),
                pltpu.VMEM((2 * rows, cells), BF16),
                pltpu.VMEM(flat, BF16),
                pltpu.VMEM(tiles, BF16),
                pltpu.VMEM(tiles, BF16),
                pltpu.VMEM(flat, BF16),
                pltpu.SemaphoreType.DMA((6 + PARTS,)),
                pltpu.SemaphoreType.DMA((4 * PARTS,)),
                pltpu.SemaphoreType.DMA((4 * PARTS,)),
                pltpu.SemaphoreType.DMA((PASSED,)),
                pltpu.SemaphoreType.DMA((2, PARTS)),
                pltpu.SemaphoreType.DMA((2, PARTS)),
                pltpu.SemaphoreType.DMA((2, JOBS)),
                pltpu.SemaphoreType.DMA((2, JOBS)),
                pltpu.SemaphoreType.REGULAR,
                pltpu.SemaphoreType.REGULAR,
            ],
            compiler_params=pltpu.CompilerParams(
                collective_id=0, has_side_effects=True, vmem_limit_bytes=48 * 1024 * 1024
            ),
            cost_estimate=pl.CostEstimate(
                flops=1_600_000_000, bytes_accessed=2_000_000, transcendentals=0
            ),
        )(
            *(
                pltpu.with_memory_space_constraint(x, pltpu.HBM)
                for x in (
                    echo_field,
                    range_chirp,
                    azimuth_filter,
                    shifts,
                    tap_index,
                    taps_table.T,
                    trig,
                )
            )
        )

    placed = (P(None, "az", "rg"), P(), P(None, "az", "rg"), P("az"), P("az"), P())
    return jax.shard_map(
        local, mesh=mesh, in_specs=placed, out_specs=P(None, "az", "rg"), check_vma=False
    )
```
